256 devices in a mesh: fsdp: 8 (over y_hi, x), context: 32 (over z, y_lo, core).
Axes of the slice: x: 4, y: 4 (y_hi: 2, y_lo: 2; y = y_hi * 2 + y_lo), z: 8, core: 2. Of those that a mesh axis runs over, the one named last changes fastest.
Arguments:
- inputs: bfloat16 [8, 4096, 8192], P('fsdp', 'context'), may hold values from -6 to 6
- queries: bfloat16 [8, 4096, 4096], P('fsdp', 'context'), may hold values from -70 to 70, as said below
- values: bfloat16 [8, 4096, 512], P('fsdp', 'context'), may hold values from -6 to 6
- output_gradient: bfloat16 [8, 4096, 4096], P('fsdp', 'context'), may hold values from -6 to 6
- key_base_weight: bfloat16 [8192, 512], P('fsdp'), may hold values from -0.0625 to 0.0625
- adapter_down: bfloat16 [8192, 64], P('fsdp'), may hold values from -0.0625 to 0.0625
- adapter_up: bfloat16 [64, 512], P(None, 'fsdp'), may hold values from -0.75 to 0.75
- span_slot_index: int32 [8, 64], P('fsdp'), may hold values from 0 to 63, each once within a row
- segment_document: int32 [8, 4096], P('fsdp'), may hold values from 0 to 31, never falling along the last dimension, each value on 1 to 1024 neighbouring positions
Outputs:
- query_grad: bfloat16 [8, 4096, 4096], P('fsdp', 'context')
- value_grad: bfloat16 [8, 4096, 512], P('fsdp', 'context')
- input_gradient: bfloat16 [8, 4096, 8192], P('fsdp', 'context')
- down_grad: float32 [8192, 64], P('fsdp')
- up_grad: float32 [64, 512], P(None, 'fsdp')
The draws below stay inside these ranges and needn't reach their ends.
Inputs may be any that keep to these rules, and one draw needn't show every extreme that they name: `queries`: in the shown draw standard normal clipped to 6; rows may carry scales up to fortyfold.
All inputs are finite; a program needn't handle non-finite values.
Results may differ from the reference program's by a relative error of at most 0.04.
Values may be sent and summed in bfloat16 or wider, within the bound.
A program may use at most 256 MiB of HBM per device.

```python
import math
import jax
import jax.numpy as jnp
import numpy as np
from jax import lax

MODEL_WIDTH = 8192
QUERY_HEADS = 32
KEY_VALUE_HEADS = 4
HEAD_SIZE = 128
ADAPTER_RANK = 64
CH = 64
KEY_FEATURES = 512
SEQS = 8
L = 4096
DOC_MAX = 1024
DOCS = 32
N_CONTEXT = 32


def draw_queries(key, part):
    key = jax.random.fold_in(key, 11)
    shape = (SEQS, 2 * CH * N_CONTEXT, QUERY_HEADS * HEAD_SIZE)
    entries = jnp.clip(jax.random.normal(key, shape, jnp.float32), -6.0, 6.0)
    return entries.astype(jnp.bfloat16)


def block_scale(key, extent, cuts, least, top_value):
    def one(dim, blocks):
        draws = jax.random.uniform(jax.random.fold_in(jax.random.fold_in(key, 6), dim), (blocks,), jnp.float32, least / len(cuts), top_value / len(cuts))
        return jnp.repeat(jnp.exp(draws), extent[dim] // blocks).reshape((-1,) + (1,) * (len(extent) - dim - 1))

    gain = one(*cuts[0])
    for cut in cuts[1:]:
        gain = gain * one(*cut)
    return gain


def length_profile(number_of, total, limit, skew):
    portions = [(1 << 20) // math.isqrt(grade ** skew) + 1 for grade in range(2, number_of + 1)]
    spare, holding = total - limit - (number_of - 1), [1] * (number_of - 1)
    while spare > 0:
        free = [i for i in range(number_of - 1) if holding[i] < limit]
        mass, remaining = sum([portions[i] for i in free]), spare
        for i in free:
            extra = min(limit - holding[i], max(1, remaining * portions[i] // mass), spare)
            holding[i] = holding[i] + extra
            spare = spare - extra
    return np.array([limit] + holding)


def ragged_sizes(key, count, total, most, skew):
    if count == 2:
        one = jax.random.randint(key, (), max(1, total - most), min(most, total - 1) + 1)
        return jnp.stack([one, total - one])
    tallies = jnp.asarray(length_profile(count, total, most, skew), jnp.int32)
    couples = (count - 1) // 2
    source_of, receiver = tallies[1:1 + 2 * couples:2], tallies[2:2 + 2 * couples:2]
    margin = jnp.minimum(source_of - 1, most - receiver)
    shifted = jax.random.randint(jax.random.fold_in(key, 1), (couples,), 0, 1 << 20) % (margin + 1)
    tallies = tallies.at[1:1 + 2 * couples:2].set(source_of - shifted).at[2:2 + 2 * couples:2].set(receiver + shifted)
    return tallies[jax.random.permutation(jax.random.fold_in(key, 2), count)]


def bell_draw(rng, dims, scale, reach, shards=(), kind=jnp.bfloat16):
    level = block_scale(rng, dims, shards, -0.22, 0.18) if shards else 1.0
    result = jax.random.normal(rng, dims, jnp.float32) * scale * level
    return jnp.minimum(jnp.maximum(result, -reach), reach).astype(kind)


def setup_inputs(seed: int = 0) -> dict:
    seeds = jax.random.split(jax.random.key(seed), 10)
    return {
        "inputs": bell_draw(seeds[0], (SEQS, L, MODEL_WIDTH), 1.0, 6.0, ((0, 8), (1, 32))),
        "queries": draw_queries(jax.random.fold_in(seeds[9], 71), 0),
        "values": bell_draw(seeds[2], (SEQS, L, KEY_FEATURES), 1.0, 6.0, ((0, 8), (1, 32))),
        "output_gradient": bell_draw(seeds[3], (SEQS, L, QUERY_HEADS * HEAD_SIZE), 1.0, 6.0, ((0, 8), (1, 32))),
        "key_base_weight": bell_draw(seeds[4], (MODEL_WIDTH, KEY_FEATURES), MODEL_WIDTH ** -0.5, 0.0625, ((0, 8),)),
        "adapter_down": bell_draw(seeds[5], (MODEL_WIDTH, ADAPTER_RANK), MODEL_WIDTH ** -0.5, 0.0625, ((0, 8),)),
        "adapter_up": bell_draw(seeds[6], (ADAPTER_RANK, KEY_FEATURES), ADAPTER_RANK ** -0.5, 0.75, ((1, 8),)),
        "span_slot_index": jax.vmap(lambda own: jax.random.permutation(own, 2 * N_CONTEXT))(jax.random.split(seeds[7], SEQS)).reshape((SEQS, 2 * N_CONTEXT)).astype(jnp.int32),
        "segment_document": jax.vmap(lambda own: jnp.searchsorted(jnp.cumsum(ragged_sizes(own, DOCS, L, DOC_MAX, 2)), jnp.arange(L), side="right"))(jax.random.split(seeds[8], SEQS)).reshape((SEQS, L)).astype(jnp.int32),
    }


ADAPTER_SCALE = 0.5
NEGATIVE_FILL = -1e+30

def span_terms(query_row_block, gradient_row_list, query_pos, query_doc, key_row_block, value_row_block, key_pos, key_doc):
    query_groups = QUERY_HEADS // KEY_VALUE_HEADS
    inv_root = 1.0 / math.sqrt(HEAD_SIZE)
    query_head_split = query_row_block.astype(jnp.float32).reshape(-1, KEY_VALUE_HEADS, query_groups, HEAD_SIZE)
    gradient_heads = gradient_row_list.astype(jnp.float32).reshape(-1, KEY_VALUE_HEADS, query_groups, HEAD_SIZE)
    key_head_split = key_row_block.astype(jnp.float32).reshape(-1, KEY_VALUE_HEADS, HEAD_SIZE)
    value_head_split = value_row_block.astype(jnp.float32).reshape(-1, KEY_VALUE_HEADS, HEAD_SIZE)
    allowed = (query_doc[:, None] == key_doc[None, :]) & (key_pos[None, :] <= query_pos[:, None])
    scores = jnp.einsum('qhgd,khd->hgqk', query_head_split, key_head_split) * inv_root
    scores = jnp.where(allowed, scores, NEGATIVE_FILL)
    peak_now = lax.optimization_barrier(jnp.max(scores, axis=-1, keepdims=True))
    normalizer = lax.optimization_barrier(jnp.sum(jnp.where(allowed, jnp.exp(scores - peak_now), 0.0), axis=-1, keepdims=True))
    log_norm = peak_now + jnp.log(normalizer)
    probability = jnp.where(allowed, jnp.exp(scores - log_norm), 0.0)
    grad_prob = jnp.einsum('qhgd,khd->hgqk', gradient_heads, value_head_split)
    row_terms = lax.optimization_barrier(jnp.sum(probability * grad_prob, axis=-1, keepdims=True))
    prob_low = lax.optimization_barrier(probability.astype(jnp.bfloat16)).astype(jnp.float32)
    dscore = lax.optimization_barrier((probability * (grad_prob - row_terms) * inv_root).astype(jnp.bfloat16)).astype(jnp.float32)
    query_part = jnp.einsum('hgqk,khd->qhgd', dscore, key_head_split)
    key_part = jnp.einsum('hgqk,qhgd->khd', dscore, query_head_split)
    value_part = jnp.einsum('hgqk,qhgd->khd', prob_low, gradient_heads)
    key_total_count = key_row_block.shape[0]
    both = jnp.concatenate([key_part.reshape(key_total_count, -1), value_part.reshape(key_total_count, -1)], axis=1)
    return (query_part.reshape(query_row_block.shape[0], -1), both)

def single_sequence(inputs, queries, values, output_gradient, span_listing, document_index, key_base_weight, adapter_down, adapter_up):
    length = inputs.shape[0]
    kv_width = values.shape[1]
    row_ids = jnp.arange(length, dtype=jnp.int32)
    positions = span_listing[row_ids // CH] * CH + row_ids % CH
    inverse = jnp.zeros((length,), jnp.int32).at[positions].set(row_ids)
    reduced_rank_input = jnp.dot(inputs, adapter_down, preferred_element_type=jnp.float32).astype(jnp.bfloat16)
    key_matrix = (jnp.dot(inputs, key_base_weight, preferred_element_type=jnp.float32) + ADAPTER_SCALE * jnp.dot(reduced_rank_input, adapter_up, preferred_element_type=jnp.float32)).astype(jnp.bfloat16)
    key_nat = key_matrix[inverse]
    value_nat = values[inverse]
    query_nat = queries[inverse]
    grad_nat = output_gradient[inverse]
    window = DOC_MAX + CH

    def device_step(carry, device):
        sums, query_acc = carry
        partial_sums = jnp.zeros((length, 2 * kv_width), jnp.float32)
        for half_index in range(2):
            first = (span_listing[2 * device + half_index] * CH).astype(jnp.int32)
            begin = jnp.clip(first + CH - window, 0, length - window).astype(jnp.int32)
            query_pos = first + jnp.arange(CH, dtype=jnp.int32)
            key_pos = begin + jnp.arange(window, dtype=jnp.int32)
            query_part, both = span_terms(lax.dynamic_slice_in_dim(query_nat, first, CH, 0), lax.dynamic_slice_in_dim(grad_nat, first, CH, 0), query_pos, document_index[query_pos], lax.dynamic_slice_in_dim(key_nat, begin, window, 0), lax.dynamic_slice_in_dim(value_nat, begin, window, 0), key_pos, document_index[key_pos])
            query_acc = lax.dynamic_update_slice_in_dim(query_acc, query_part.astype(jnp.bfloat16), first, 0)
            previous = lax.dynamic_slice_in_dim(partial_sums, begin, window, 0)
            partial_sums = lax.dynamic_update_slice_in_dim(partial_sums, previous + both, begin, 0)
        rounded = lax.optimization_barrier(partial_sums.astype(jnp.bfloat16)).astype(jnp.float32)
        return ((sums + rounded, query_acc), None)
    start_state = (jnp.zeros((length, 2 * kv_width), jnp.float32), jnp.zeros(queries.shape, jnp.bfloat16))
    (sums, query_acc), _ = lax.scan(device_step, start_state, jnp.arange(N_CONTEXT, dtype=jnp.int32))
    key_gradient = sums[:, :kv_width].astype(jnp.bfloat16)[positions]
    value_grad = sums[:, kv_width:].astype(jnp.bfloat16)[positions]
    query_grad = query_acc[positions]
    key_lifted = jnp.dot(key_gradient, adapter_up.T, preferred_element_type=jnp.float32).astype(jnp.bfloat16)
    input_gradient = (jnp.dot(key_gradient, key_base_weight.T, preferred_element_type=jnp.float32) + ADAPTER_SCALE * jnp.dot(key_lifted, adapter_down.T, preferred_element_type=jnp.float32)).astype(jnp.bfloat16)
    down_portion = ADAPTER_SCALE * jnp.dot(inputs.T, key_lifted, preferred_element_type=jnp.float32)
    up_portion = ADAPTER_SCALE * jnp.dot(reduced_rank_input.T, key_gradient, preferred_element_type=jnp.float32)
    return (query_grad, value_grad, input_gradient, down_portion, up_portion)

def reference(inputs, queries, values, output_gradient, key_base_weight, adapter_down, adapter_up, span_slot_index, segment_document):

    def per_sequence(listed_entries):
        return single_sequence(listed_entries[0], listed_entries[1], listed_entries[2], listed_entries[3], listed_entries[4], listed_entries[5], key_base_weight, adapter_down, adapter_up)
    query_grad, value_grad, input_gradient, down_parts, up_parts = lax.map(per_sequence, (inputs, queries, values, output_gradient, span_slot_index, segment_document))
    return (query_grad, value_grad, input_gradient, lax.optimization_barrier(jnp.sum(down_parts, axis=0)), lax.optimization_barrier(jnp.sum(up_parts, axis=0)))
```

```python
import functools
import math

import jax
import jax.numpy as jnp
from jax import lax
from jax.experimental import pallas as pl
from jax.experimental.pallas import tpu as pltpu
from jax.sharding import PartitionSpec as P

QUERY_HEADS = 32
KEY_VALUE_HEADS = 4
HEAD_SIZE = 128
GROUPS = QUERY_HEADS // KEY_VALUE_HEADS
SPAN = 64
ADAPTER_SCALE = 0.5
NEGATIVE_FILL = -1e30
KEY_TILE = 256
MESH = pl.DeviceIdType.MESH
ANY = pl.BlockSpec(memory_space=pl.ANY)
VMEM = pl.BlockSpec(memory_space=pltpu.VMEM)
SMEM = pl.BlockSpec(memory_space=pltpu.SMEM)


def at(start, size):
    return pl.ds(pl.multiple_of(start, size), size)


class Place:
    def __init__(self, zs):
        self.zs = zs
        self.fsdp = lax.axis_index("fsdp")
        self.context = lax.axis_index("context")
        self.y_hi, self.x = lax.div(self.fsdp, 4), lax.rem(self.fsdp, 4)
        self.z, self.member = lax.div(self.context, 4), lax.rem(self.context, 4)
        self.y_lo, self.core = lax.div(self.member, 2), lax.rem(self.member, 2)

    def row(self, y_hi, x):
        return y_hi * 4 + lax.rem(x, 4)

    def at_x(self, step):
        return {"fsdp": self.row(self.y_hi, self.x + step), "context": self.context}

    def across_y(self):
        return {
            "fsdp": self.row(1 - self.y_hi, self.x),
            "context": self.z * 4 + (1 - self.y_lo) * 2 + self.core,
        }

    def other_y_lo(self):
        return self.of_context(self.z * 4 + (1 - self.y_lo) * 2 + self.core)

    def sibling(self):
        return self.of_context(self.z * 4 + self.y_lo * 2 + 1 - self.core)

    def of_context(self, context):
        return {"fsdp": self.fsdp, "context": context}

    def fellow(self, k):
        return lax.rem(self.member + k, 4)

    def at_fellow(self, k):
        return self.of_context(self.z * 4 + self.fellow(k))

    def z_at(self, step):
        return lax.rem(self.z + step + self.zs, self.zs)

    def at_z(self, step):
        return self.of_context(self.z_at(step) * 4 + self.member)


def greet(partners):
    barrier = pltpu.get_barrier_semaphore()
    for partner in partners:
        pl.semaphore_signal(barrier, inc=1, device_id=partner, device_id_type=MESH)
    pl.semaphore_wait(barrier, len(partners))


class Sender:
    def __init__(self, send_sems, recv_sems):
        self.send_sems, self.recv_sems, self.copies = send_sems, recv_sems, []

    def send(self, src, dst, device):
        k = len(self.copies)
        assert k < self.send_sems.shape[0]
        copy = pltpu.make_async_remote_copy(
            src_ref=src,
            dst_ref=dst,
            send_sem=self.send_sems.at[k],
            recv_sem=self.recv_sems.at[k],
            device_id=device,
            device_id_type=MESH,
        )
        copy.start()
        self.copies.append(copy)
        return copy

    def finish(self):
        for copy in self.copies:
            copy.wait_send()


def ring_gather(place, sender, buffer, rows):
    half = place.zs // 2
    last_right = last_left = None
    for step in range(half):
        if last_right is not None:
            last_right.wait_recv()
            last_left.wait_recv()
        right_at, left_at = place.z_at(-step) * rows, place.z_at(step) * rows
        if step < half - 1:
            right_rows, left_rows = at(right_at, rows), at(left_at, rows)
        else:
            cut = rows // 2
            right_rows, left_rows = at(right_at, cut), at(left_at + cut, cut)
        last_right = sender.send(buffer.at[right_rows], buffer.at[right_rows], place.at_z(1))
        last_left = sender.send(buffer.at[left_rows], buffer.at[left_rows], place.at_z(-1))
        yield
    last_right.wait_recv()
    last_left.wait_recv()


def weights_kernel(
    zs, w_ref, q_ref, g_ref, v_ref, wf_ref, qg_ref, gg_ref, vg_ref, send_sems, recv_sems, own_sems
):
    place = Place(zs)
    tokens = q_ref.shape[0]
    shard = w_ref.shape[0]
    piece, part = shard // 2, shard // 4
    width = GROUPS * HEAD_SIZE
    member = place.member
    owns = [
        pltpu.make_async_copy(w_ref, wf_ref.at[at(place.fsdp * shard, shard)], own_sems.at[0]),
        pltpu.make_async_copy(
            q_ref.at[:, at(member * width, width)], qg_ref.at[at(member * tokens, tokens)], own_sems.at[1]
        ),
        pltpu.make_async_copy(
            g_ref.at[:, at(member * width, width)], gg_ref.at[at(member * tokens, tokens)], own_sems.at[2]
        ),
        pltpu.make_async_copy(
            v_ref.at[:, at(member * HEAD_SIZE, HEAD_SIZE)],
            vg_ref.at[at((place.z * 4 + member) * tokens, tokens)],
            own_sems.at[3],
        ),
    ]
    for own in owns:
        own.start()
    right, left, across, sibling = place.at_x(1), place.at_x(3), place.across_y(), place.sibling()
    greet([right, left, across] + [place.at_fellow(k) for k in (1, 2, 3)] + [place.at_z(1), place.at_z(-1)])
    sender = Sender(send_sems, recv_sems)
    send = sender.send

    value_copies = []
    for k in (1, 2, 3):
        fellow = place.fellow(k)
        value_copies.append(
            send(
                v_ref.at[:, at(fellow * HEAD_SIZE, HEAD_SIZE)],
                vg_ref.at[at((place.z * 4 + member) * tokens, tokens)],
                place.at_fellow(k),
            )
        )

    def rows_of(y_hi, x, offset, size):
        return wf_ref.at[at(place.row(y_hi, x) * shard + place.core * piece + offset, size)]

    y_hi, other, x = place.y_hi, 1 - place.y_hi, place.x
    own_piece = w_ref.at[at(place.core * piece, piece)]
    landing = rows_of(y_hi, x, 0, piece)
    to_right = send(own_piece, landing, right)
    to_left = send(own_piece, landing, left)
    to_across = send(own_piece, landing, across)
    head_copies = []
    for k in (2, 3, 1):
        fellow = place.fellow(k)
        for src, dst in ((q_ref, qg_ref), (g_ref, gg_ref)):
            head_copies.append(
                send(
                    src.at[:, at(fellow * width, width)],
                    dst.at[at(member * tokens, tokens)],
                    place.at_fellow(k),
                )
            )
    for copy in value_copies:
        copy.wait_recv()
    owns[3].wait()
    ring = ring_gather(place, sender, vg_ref, 4 * tokens)
    next(ring)

    shared = []

    def share(block):
        shared.append(send(block, block, sibling))

    to_right.wait_recv()
    half_right = send(rows_of(y_hi, x + 3, 0, part), rows_of(y_hi, x + 3, 0, part), right)
    to_left.wait_recv()
    half_left = send(rows_of(y_hi, x + 1, part, part), rows_of(y_hi, x + 1, part, part), left)
    share(rows_of(y_hi, x + 3, 0, piece))
    share(rows_of(y_hi, x + 1, 0, piece))
    to_across.wait_recv()
    block = rows_of(other, x, 0, piece)
    on_right = send(block, block, right)
    on_left = send(block, block, left)
    share(block)
    next(ring, None)
    half_right.wait_recv()
    block = rows_of(y_hi, x + 2, 0, part)
    first_across = send(block, block, across)
    share(block)
    half_left.wait_recv()
    block = rows_of(y_hi, x + 2, part, part)
    second_across = send(block, block, across)
    share(block)
    for _ in ring:
        pass
    on_right.wait_recv()
    share(rows_of(other, x + 3, 0, piece))
    on_left.wait_recv()
    share(rows_of(other, x + 1, 0, piece))
    first_across.wait_recv()
    share(rows_of(other, x + 2, 0, part))
    second_across.wait_recv()
    share(rows_of(other, x + 2, part, part))
    for copy in head_copies + shared:
        copy.wait_recv()
    sender.finish()
    for own in owns[:3]:
        own.wait()


def keys_kernel(zs, k_ref, kg_ref, send_sems, recv_sems, own_sem):
    place = Place(zs)
    tokens = k_ref.shape[0]
    member = place.member
    mine = at((place.z * 4 + member) * tokens, tokens)
    own = pltpu.make_async_copy(k_ref.at[:, at(member * HEAD_SIZE, HEAD_SIZE)], kg_ref.at[mine], own_sem)
    own.start()
    greet([place.at_fellow(k) for k in (1, 2, 3)] + [place.at_z(1), place.at_z(-1)])
    sender = Sender(send_sems, recv_sems)
    copies = []
    for k in (1, 2, 3):
        fellow = place.fellow(k)
        copies.append(
            sender.send(
                k_ref.at[:, at(fellow * HEAD_SIZE, HEAD_SIZE)], kg_ref.at[mine], place.at_fellow(k)
            )
        )
    for copy in copies:
        copy.wait_recv()
    own.wait()
    for _ in ring_gather(place, sender, kg_ref, 4 * tokens):
        pass
    sender.finish()


def attention_kernel(
    slot_ref,
    first_ref,
    inverse_ref,
    pos_ref,
    start_ref,
    q_ref,
    g_ref,
    k_ref,
    v_ref,
    dq_ref,
    dkv_ref,
    keys,
    values,
    totals,
    scores,
    grads,
):
    inv_root = 1.0 / math.sqrt(HEAD_SIZE)
    lanes = GROUPS * SPAN
    spans = inverse_ref.shape[0]

    @pl.loop(0, spans)
    def _(n):
        src, dst = at(inverse_ref[n] * SPAN, SPAN), at(n * SPAN, SPAN)
        keys[dst, :] = k_ref[src, :]
        values[dst, :] = v_ref[src, :]
        totals[dst, :] = jnp.zeros((SPAN, 2 * HEAD_SIZE), jnp.float32)

    @pl.loop(0, slot_ref.shape[0])
    def _(i):
        slot, first = slot_ref[i], first_ref[i]
        own = at(i * SPAN, SPAN)
        q_rows = jnp.concatenate(
            [q_ref[own, g * HEAD_SIZE : (g + 1) * HEAD_SIZE] for g in range(GROUPS)], axis=0
        )
        g_rows = jnp.concatenate(
            [g_ref[own, g * HEAD_SIZE : (g + 1) * HEAD_SIZE] for g in range(GROUPS)], axis=0
        )
        q_pos, q_start = pos_ref[pl.ds(i, 1), :], start_ref[pl.ds(i, 1), :]
        low_tile = lax.div(first * SPAN, KEY_TILE)
        tiles = lax.div(slot * SPAN, KEY_TILE) - low_tile + 1

        def rows_at(t):
            return at((low_tile + t) * KEY_TILE, KEY_TILE)

        def peak_step(t, peak):
            rows = rows_at(t)
            raw = lax.dot_general(
                keys[rows, :], q_rows, (((1,), (1,)), ((), ())), preferred_element_type=jnp.float32
            )
            key_pos = (low_tile + t) * KEY_TILE + lax.broadcasted_iota(jnp.int32, (KEY_TILE, lanes), 0)
            raw = jnp.where((key_pos >= q_start) & (key_pos <= q_pos), raw * inv_root, NEGATIVE_FILL)
            scores[t] = raw
            return jnp.maximum(peak, jnp.max(raw, axis=0, keepdims=True))

        peak = lax.fori_loop(0, tiles, peak_step, jnp.full((1, lanes), NEGATIVE_FILL, jnp.float32))

        def sum_step(t, carry):
            normalizer, weighted = carry
            grad_prob = lax.dot_general(
                values[rows_at(t), :], g_rows, (((1,), (1,)), ((), ())), preferred_element_type=jnp.float32
            )
            weights = jnp.exp(scores[t] - peak)
            scores[t] = weights
            grads[t] = grad_prob
            return (
                normalizer + jnp.sum(weights, axis=0, keepdims=True),
                weighted + jnp.sum(weights * grad_prob, axis=0, keepdims=True),
            )

        zero = jnp.zeros((1, lanes), jnp.float32)
        normalizer, weighted = lax.fori_loop(0, tiles, sum_step, (zero, zero))
        inverse = 1.0 / normalizer
        row_terms = weighted * inverse

        def grad_step(t, dq):
            rows = rows_at(t)
            probability = scores[t] * inverse
            dscore = (probability * (grads[t] - row_terms) * inv_root).astype(jnp.bfloat16)
            prob_low = probability.astype(jnp.bfloat16)
            totals[rows, :HEAD_SIZE] += jnp.dot(dscore, q_rows, preferred_element_type=jnp.float32)
            totals[rows, HEAD_SIZE:] += jnp.dot(prob_low, g_rows, preferred_element_type=jnp.float32)
            return dq + lax.dot_general(
                keys[rows, :], dscore, (((0,), (0,)), ((), ())), preferred_element_type=jnp.float32
            )

        dq = lax.fori_loop(0, tiles, grad_step, jnp.zeros((HEAD_SIZE, lanes), jnp.float32))
        dq = dq.T.astype(jnp.bfloat16)
        for g in range(GROUPS):
            dq_ref[own, g * HEAD_SIZE : (g + 1) * HEAD_SIZE] = dq[g * SPAN : (g + 1) * SPAN]

    @pl.loop(0, spans)
    def _(n):
        dkv_ref[at(inverse_ref[n] * SPAN, SPAN), :] = totals[at(n * SPAN, SPAN), :].astype(jnp.bfloat16)


REDUCE_CUTS = 2


def reduce_plan(zs):
    half = zs // 2
    return [(1, 0, half), (-1, 1, half), (-1, 0, half - 1), (1, 1, half - 1)]


def reduce_kernel(zs, dkv_ref, dqg_ref, dq_ref, kg_ref, vg_ref, out, held, done, send_sems, recv_sems, own_sems):
    place = Place(zs)
    tokens = dq_ref.shape[0]
    width = GROUPS * HEAD_SIZE
    member = place.member
    rows = 4 * tokens
    cut = rows // REDUCE_CUTS
    own_query = pltpu.make_async_copy(
        dqg_ref.at[at(member * tokens, tokens)], dq_ref.at[:, at(member * width, width)], own_sems.at[0]
    )
    own_query.start()
    greet([place.at_fellow(k) for k in (1, 2, 3)] + [place.at_z(1), place.at_z(-1)])
    sender = Sender(send_sems, recv_sems)
    plan = reduce_plan(zs)
    last = {}
    slot = 0
    query_copies = []
    for step in range(zs // 2):
        for piece in range(REDUCE_CUTS):
            for chain, (direction, column, hops) in enumerate(plan):
                if step >= hops:
                    continue
                columns = slice(column * HEAD_SIZE, (column + 1) * HEAD_SIZE)
                destination = place.z_at(direction * (hops - step))
                mine = dkv_ref[at(destination * rows + piece * cut, cut), columns]
                if step > 0:
                    copy, before = last[chain, piece]
                    copy.wait_recv()
                    mine = (mine.astype(jnp.float32) + held[before].astype(jnp.float32)).astype(jnp.bfloat16)
                out[slot] = mine
                last[chain, piece] = (
                    sender.send(out.at[slot], held.at[slot], place.at_z(direction)),
                    slot,
                )
                slot += 1
        if step == 0:
            for k in (2, 3, 1):
                fellow = place.fellow(k)
                query_copies.append(
                    sender.send(
                        dqg_ref.at[at(fellow * tokens, tokens)],
                        dq_ref.at[:, at(member * width, width)],
                        place.at_fellow(k),
                    )
                )
    for piece in range(REDUCE_CUTS):
        for column in range(2):
            columns = slice(column * HEAD_SIZE, (column + 1) * HEAD_SIZE)
            total = dkv_ref[at(place.z * rows + piece * cut, cut), columns].astype(jnp.float32)
            for chain, (direction, its_column, hops) in enumerate(plan):
                if its_column == column and hops:
                    copy, before = last[chain, piece]
                    copy.wait_recv()
                    total = total + held[before].astype(jnp.float32)
            done[column, piece * cut : (piece + 1) * cut, :] = total.astype(jnp.bfloat16)
    sums = []
    for column, target in ((0, kg_ref), (1, vg_ref)):
        own = pltpu.make_async_copy(
            done.at[column, at(member * tokens, tokens)],
            target.at[:, at(member * HEAD_SIZE, HEAD_SIZE)],
            own_sems.at[1 + column],
        )
        own.start()
        sums.append(own)
    copies = []
    for k in (2, 3, 1):
        for column, target in ((0, kg_ref), (1, vg_ref)):
            copies.append(
                sender.send(
                    done.at[column, at(place.fellow(k) * tokens, tokens)],
                    target.at[:, at(member * HEAD_SIZE, HEAD_SIZE)],
                    place.at_fellow(k),
                )
            )
    for copy in copies + query_copies:
        copy.wait_recv()
    sender.finish()
    for own in sums + [own_query]:
        own.wait()


def adapter_kernel(
    zs, part_ref, total_ref, pair_in, row_out, row_in, y_out, y_in, z_out, z_in, lo_out, lo_in, send_sems, recv_sems
):
    place = Place(zs)
    lanes = part_ref.shape[3] - 128
    cut = lanes // zs
    sibling, across, other_lo = place.sibling(), place.across_y(), place.other_y_lo()
    partners = [place.at_x(k) for k in (1, 2, 3)] + [across, other_lo]
    partners += [place.at_z(k) for k in range(1, zs)]
    partners += [
        place.of_context(place.z_at(k) * 4 + place.y_lo * 2 + 1 - place.core) for k in range(zs)
    ]
    greet(partners)
    sender = Sender(send_sems, recv_sems)
    send = sender.send
    copy = send(part_ref.at[:, 1 - place.core], pair_in, sibling)
    copy.wait_recv()
    row_out[...] = (
        part_ref[:, pl.ds(place.core, 1)][:, 0].astype(jnp.float32) + pair_in[...].astype(jnp.float32)
    ).astype(jnp.bfloat16)
    copies = []
    for k in (2, 1, 3):
        for y_hi in range(2):
            copies.append(
                send(
                    row_out.at[place.row(y_hi, place.x + k)], row_in.at[k - 1, y_hi], place.at_x(k)
                )
            )
    for copy in copies:
        copy.wait_recv()

    def over_x(y_hi):
        total = row_out[place.row(y_hi, place.x)].astype(jnp.float32)
        for k in range(3):
            total = total + row_in[k, y_hi].astype(jnp.float32)
        return total

    y_out[...] = over_x(1 - place.y_hi)
    copy = send(y_out, y_in, across)
    mine = over_x(place.y_hi)
    copy.wait_recv()
    mine = mine + y_in[...]
    for j in range(zs):
        z_out[j, 0] = mine[:, j * cut : (j + 1) * cut]
        z_out[j, 1] = mine[:, lanes:]
    copies = []
    for k in sorted(range(1, zs), key=lambda k: -min(k, zs - k)):
        copies.append(send(z_out.at[place.z_at(k)], z_in.at[k - 1], place.at_z(k)))
    for copy in copies:
        copy.wait_recv()
    chunk = z_out[place.z]
    for k in range(zs - 1):
        chunk = chunk + z_in[k]
    lo_out[...] = chunk
    copy = send(lo_out, lo_in, other_lo)
    copy.wait_recv()
    chunk = chunk + lo_in[...]
    total_ref[pl.ds(place.core, 1), pl.ds(place.z, 1)] = chunk[0][None, None]
    total_ref[pl.ds(place.core, 1), zs : zs + 1] = chunk[1][None, None]
    copies = [
        send(total_ref.at[place.core, zs], total_ref.at[place.core, zs], sibling),
    ]
    block = total_ref.at[place.core, place.z]
    for k in sorted(range(zs), key=lambda k: -min(k, zs - k)):
        if k:
            copies.append(send(block, block, place.at_z(k)))
        copies.append(
            send(block, block, place.of_context(place.z_at(k) * 4 + place.y_lo * 2 + 1 - place.core))
        )
    for copy in copies:
        copy.wait_recv()
    sender.finish()


def dma(count):
    return pltpu.SemaphoreType.DMA((count,))


def params(collective_id=None):
    if collective_id is None:
        return pltpu.CompilerParams(vmem_limit_bytes=56 << 20)
    return pltpu.CompilerParams(
        vmem_limit_bytes=48 << 20, collective_id=collective_id, has_side_effects=True
    )


def body(
    zs,
    inputs,
    queries,
    values,
    output_gradient,
    key_base_weight,
    adapter_down,
    adapter_up,
    span_slot_index,
    segment_document,
):
    bf16, f32, i32 = jnp.bfloat16, jnp.float32, jnp.int32
    rows_in = inputs[0]
    tokens, model = rows_in.shape
    shard, kv_width = key_base_weight.shape
    rank = adapter_down.shape[1]
    length = segment_document.shape[1]
    width = GROUPS * HEAD_SIZE
    half = zs // 2

    up_block = jnp.pad(adapter_up, ((0, shard - rank), (0, 0)))
    packed = jnp.concatenate([key_base_weight, adapter_down, up_block], axis=1)
    packed_width = packed.shape[1]
    full, query_group, gradient_group, value_all = pl.pallas_call(
        functools.partial(weights_kernel, zs),
        out_shape=(
            jax.ShapeDtypeStruct((model, packed_width), bf16),
            jax.ShapeDtypeStruct((4 * tokens, width), bf16),
            jax.ShapeDtypeStruct((4 * tokens, width), bf16),
            jax.ShapeDtypeStruct((length, HEAD_SIZE), bf16),
        ),
        in_specs=[ANY] * 4,
        out_specs=(ANY,) * 4,
        scratch_shapes=[dma(27 + 2 * half), dma(27 + 2 * half), dma(4)],
        compiler_params=params(0),
        name="gather_weights",
    )(packed, queries[0], output_gradient[0], values[0])

    projected = jnp.dot(rows_in, full, preferred_element_type=f32)
    low_rank = projected[:, kv_width : kv_width + rank].astype(bf16)
    up_blocks = full.reshape(8, shard, packed_width)[:, :rank, kv_width + rank :]
    complete_up = up_blocks.transpose(1, 0, 2).reshape(rank, kv_width)
    key_matrix = (
        projected[:, :kv_width]
        + ADAPTER_SCALE * jnp.dot(low_rank, complete_up, preferred_element_type=f32)
    ).astype(bf16)

    key_all = pl.pallas_call(
        functools.partial(keys_kernel, zs),
        out_shape=jax.ShapeDtypeStruct((length, HEAD_SIZE), bf16),
        in_specs=[ANY],
        out_specs=ANY,
        scratch_shapes=[dma(3 + 2 * half), dma(3 + 2 * half), pltpu.SemaphoreType.DMA],
        compiler_params=params(1),
        name="gather_keys",
    )(key_matrix)

    listing, documents = span_slot_index[0], segment_document[0]
    spans = listing.shape[0]
    z = lax.axis_index("context") // 4
    own_spans = 4 * tokens // SPAN
    slots = lax.dynamic_slice_in_dim(listing, z * own_spans, own_spans, 0)
    span_ids = jnp.arange(spans, dtype=i32)
    inverse = jnp.sum(jnp.where(listing[None, :] == span_ids[:, None], span_ids[None, :], 0), axis=1)
    own_docs = documents.reshape(spans, SPAN)[slots]
    starts = jnp.sum((documents[None, None, :] < own_docs[:, :, None]).astype(i32), axis=2)
    positions = slots[:, None] * SPAN + jnp.arange(SPAN, dtype=i32)[None, :]
    query_grad_group, partial_sums = pl.pallas_call(
        attention_kernel,
        out_shape=(
            jax.ShapeDtypeStruct((4 * tokens, width), bf16),
            jax.ShapeDtypeStruct((length, 2 * HEAD_SIZE), bf16),
        ),
        in_specs=[SMEM] * 3 + [VMEM] * 6,
        out_specs=(VMEM, VMEM),
        scratch_shapes=[
            pltpu.VMEM((length, HEAD_SIZE), bf16),
            pltpu.VMEM((length, HEAD_SIZE), bf16),
            pltpu.VMEM((length, 2 * HEAD_SIZE), f32),
            pltpu.VMEM((1024 // KEY_TILE + 2, KEY_TILE, GROUPS * SPAN), f32),
            pltpu.VMEM((1024 // KEY_TILE + 2, KEY_TILE, GROUPS * SPAN), f32),
        ],
        compiler_params=params(),
        name="attention_gradients",
    )(
        slots,
        starts[:, 0] // SPAN,
        inverse,
        jnp.tile(positions, (1, GROUPS)),
        jnp.tile(starts, (1, GROUPS)),
        query_group,
        gradient_group,
        key_all,
        value_all,
    )

    hops = REDUCE_CUTS * sum(hops for _, _, hops in reduce_plan(zs))
    cut = 4 * tokens // REDUCE_CUTS
    query_grad, key_gradient, value_grad = pl.pallas_call(
        functools.partial(reduce_kernel, zs),
        out_shape=(
            jax.ShapeDtypeStruct((tokens, QUERY_HEADS * HEAD_SIZE), bf16),
            jax.ShapeDtypeStruct((tokens, kv_width), bf16),
            jax.ShapeDtypeStruct((tokens, kv_width), bf16),
        ),
        in_specs=[VMEM, ANY],
        out_specs=(ANY,) * 3,
        scratch_shapes=[
            pltpu.VMEM((hops, cut, HEAD_SIZE), bf16),
            pltpu.VMEM((hops, cut, HEAD_SIZE), bf16),
            pltpu.VMEM((2, 4 * tokens, HEAD_SIZE), bf16),
            dma(hops + 9),
            dma(hops + 9),
            dma(3),
        ],
        compiler_params=params(2),
        name="reduce_keys_values",
    )(partial_sums, query_grad_group)

    key_lifted = lax.dot_general(
        key_gradient, complete_up, (((1,), (1,)), ((), ())), preferred_element_type=f32
    ).astype(bf16)
    scaled_lifted = (key_lifted.astype(f32) * ADAPTER_SCALE).astype(bf16)
    stacked = jnp.concatenate([key_gradient, scaled_lifted, jnp.zeros_like(key_lifted)], axis=1)
    down_part = lax.dot_general(
        scaled_lifted, rows_in, (((0,), (0,)), ((), ())), preferred_element_type=f32
    ).astype(bf16)
    up_part = ADAPTER_SCALE * lax.dot_general(
        low_rank, key_gradient, (((0,), (0,)), ((), ())), preferred_element_type=f32
    )
    share = kv_width // 8
    down_part = down_part.reshape(2, rank // 2, 8, shard).transpose(2, 0, 1, 3)
    up_part = up_part.astype(bf16).reshape(2, rank // 2, 8, share).transpose(2, 0, 1, 3)
    up_part = jnp.pad(up_part, ((0, 0), (0, 0), (0, 0), (0, 128 - share)))
    parts = jnp.concatenate([down_part, up_part], axis=3)
    lanes = shard + 128
    chunk = shard // zs
    ranks = rank // 2
    copies = 1 + 6 + 1 + (zs - 1) + 1 + 1 + 2 * zs - 1
    totals = pl.pallas_call(
        functools.partial(adapter_kernel, zs),
        out_shape=jax.ShapeDtypeStruct((2, zs + 1, ranks, chunk), f32),
        in_specs=[VMEM],
        out_specs=VMEM,
        scratch_shapes=[
            pltpu.VMEM((8, ranks, lanes), bf16),
            pltpu.VMEM((8, ranks, lanes), bf16),
            pltpu.VMEM((3, 2, ranks, lanes), bf16),
            pltpu.VMEM((ranks, lanes), f32),
            pltpu.VMEM((ranks, lanes), f32),
            pltpu.VMEM((zs, 2, ranks, chunk), f32),
            pltpu.VMEM((zs - 1, 2, ranks, chunk), f32),
            pltpu.VMEM((2, ranks, chunk), f32),
            pltpu.VMEM((2, ranks, chunk), f32),
            dma(copies),
            dma(copies),
        ],
        compiler_params=params(3),
        name="sum_adapter_gradients",
    )(parts)
    input_gradient = lax.dot_general(
        stacked, full, (((1,), (1,)), ((), ())), preferred_element_type=f32
    ).astype(bf16)
    down_share = totals[:, :zs].transpose(1, 3, 0, 2).reshape(shard, rank)
    up_share = totals[:, zs, :, :share].reshape(rank, share)
    return (query_grad[None], value_grad[None], input_gradient[None], down_share, up_share)


def solution(mesh):
    spread, rows = P("fsdp", "context", None), P("fsdp", None)
    placed = (spread, spread, spread, spread, rows, rows, P(None, "fsdp"), rows, rows)
    return jax.shard_map(
        functools.partial(body, mesh.shape["context"] // 4),
        mesh=mesh,
        in_specs=placed,
        out_specs=(spread, spread, spread, rows, P(None, "fsdp")),
        check_vma=False,
    )
```

```python
import functools
import math

import jax
import jax.numpy as jnp
from jax import lax
from jax.experimental import pallas as pl
from jax.experimental.pallas import tpu as pltpu
from jax.sharding import PartitionSpec as P

QUERY_HEADS = 32
KEY_VALUE_HEADS = 4
HEAD_SIZE = 128
GROUPS = QUERY_HEADS // KEY_VALUE_HEADS
SPAN = 64
ADAPTER_SCALE = 0.5
NEGATIVE_FILL = -1e30
KEY_TILE = 256
MESH = pl.DeviceIdType.MESH
ANY = pl.BlockSpec(memory_space=pl.ANY)
VMEM = pl.BlockSpec(memory_space=pltpu.VMEM)
SMEM = pl.BlockSpec(memory_space=pltpu.SMEM)


def at(start, size):
    return pl.ds(pl.multiple_of(start, size), size)


class Place:
    def __init__(self, zs):
        self.zs = zs
        self.fsdp = lax.axis_index("fsdp")
        self.context = lax.axis_index("context")
        self.y_hi, self.x = lax.div(self.fsdp, 4), lax.rem(self.fsdp, 4)
        self.z, self.member = lax.div(self.context, 4), lax.rem(self.context, 4)
        self.y_lo, self.core = lax.div(self.member, 2), lax.rem(self.member, 2)

    def row(self, y_hi, x):
        return y_hi * 4 + lax.rem(x, 4)

    def at_x(self, step):
        return {"fsdp": self.row(self.y_hi, self.x + step), "context": self.context}

    def across_y(self):
        return {
            "fsdp": self.row(1 - self.y_hi, self.x),
            "context": self.z * 4 + (1 - self.y_lo) * 2 + self.core,
        }

    def other_y_lo(self):
        return self.of_context(self.z * 4 + (1 - self.y_lo) * 2 + self.core)

    def sibling(self):
        return self.of_context(self.z * 4 + self.y_lo * 2 + 1 - self.core)

    def of_context(self, context):
        return {"fsdp": self.fsdp, "context": context}

    def fellow(self, k):
        return lax.rem(self.member + k, 4)

    def at_fellow(self, k):
        return self.of_context(self.z * 4 + self.fellow(k))

    def z_at(self, step):
        return lax.rem(self.z + step + self.zs, self.zs)

    def at_z(self, step):
        return self.of_context(self.z_at(step) * 4 + self.member)


def greet(partners):
    barrier = pltpu.get_barrier_semaphore()
    for partner in partners:
        pl.semaphore_signal(barrier, inc=1, device_id=partner, device_id_type=MESH)
    pl.semaphore_wait(barrier, len(partners))


class Sender:
    def __init__(self, send_sems, recv_sems):
        self.send_sems, self.recv_sems, self.copies = send_sems, recv_sems, []

    def send(self, src, dst, device):
        k = len(self.copies)
        assert k < self.send_sems.shape[0]
        copy = pltpu.make_async_remote_copy(
            src_ref=src,
            dst_ref=dst,
            send_sem=self.send_sems.at[k],
            recv_sem=self.recv_sems.at[k],
            device_id=device,
            device_id_type=MESH,
        )
        copy.start()
        self.copies.append(copy)
        return copy

    def finish(self):
        for copy in self.copies:
            copy.wait_send()


class Ring:
    def __init__(self, place, sender, buffer, block, rows):
        self.place, self.sender, self.buffer = place, sender, buffer
        self.block, self.rows, self.stage, self.flying = block, rows, 0, ()
        self.stages = place.zs // 2

    def step(self):
        for copy in self.flying:
            copy.wait_recv()
        self.flying = ()
        if self.stage == self.stages:
            return
        right_at, left_at = self.block(self.place.z_at(-self.stage)), self.block(self.place.z_at(self.stage))
        if self.stage < self.stages - 1:
            right_rows, left_rows = at(right_at, self.rows), at(left_at, self.rows)
        else:
            cut = self.rows // 2
            right_rows, left_rows = at(right_at, cut), at(left_at + cut, cut)
        buffer, send = self.buffer, self.sender.send
        self.flying = (
            send(buffer.at[right_rows], buffer.at[right_rows], self.place.at_z(1)),
            send(buffer.at[left_rows], buffer.at[left_rows], self.place.at_z(-1)),
        )
        self.stage += 1

    def run(self):
        while self.stage < self.stages or self.flying:
            self.step()


def keys_kernel(
    zs,
    w_ref,
    d_ref,
    u_ref,
    x_hbm,
    q_ref,
    g_ref,
    v_ref,
    full_ref,
    qg_ref,
    gg_ref,
    vg_ref,
    kg_ref,
    low_ref,
    up_ref,
    full,
    inputs,
    projected,
    keys,
    send_sems,
    recv_sems,
    own_sems,
):
    place = Place(zs)
    tokens = q_ref.shape[0]
    shard, kv_width = w_ref.shape
    rank = d_ref.shape[1]
    unit = shard // 8
    width = GROUPS * HEAD_SIZE
    member = place.member
    mine = at((place.z * 4 + member) * tokens, tokens)
    columns = at(member * HEAD_SIZE, HEAD_SIZE)
    load = pltpu.make_async_copy(x_hbm, inputs, own_sems.at[0])
    load.start()
    owns = [
        pltpu.make_async_copy(
            q_ref.at[:, at(member * width, width)], qg_ref.at[at(member * tokens, tokens)], own_sems.at[1]
        ),
        pltpu.make_async_copy(
            g_ref.at[:, at(member * width, width)], gg_ref.at[at(member * tokens, tokens)], own_sems.at[2]
        ),
        pltpu.make_async_copy(v_ref.at[:, columns], vg_ref.at[mine], own_sems.at[3]),
    ]
    for own in owns:
        own.start()
    own_rows = at(place.fsdp * shard, shard)
    full[own_rows, :kv_width] = w_ref[...]
    up_rows = jnp.concatenate([u_ref[...], jnp.zeros((shard - rank, u_ref.shape[1]), jnp.bfloat16)], axis=0)
    full[own_rows, kv_width:] = jnp.concatenate([d_ref[...], up_rows], axis=1)
    projected[...] = jnp.zeros_like(projected)

    right, left, across, sibling = place.at_x(1), place.at_x(3), place.across_y(), place.sibling()
    z_up, z_down = place.at_z(1), place.at_z(-1)
    greet([right, left, across] + [place.at_fellow(k) for k in (1, 2, 3)] + [z_up, z_down])
    sender = Sender(send_sems, recv_sems)
    send = sender.send

    parity = lax.rem(place.z, 2)

    def rows_of(f, offset, size):
        begin = f * shard + place.core * 4 * unit + offset
        return full.at[pl.ds(pl.multiple_of(begin, unit // 2), size)]

    def main(f):
        return rows_of(f, parity * unit, 3 * unit)

    def pass_on(block, *devices):
        return [send(block, block, device) for device in devices]

    half = 3 * unit // 2

    def first_half(f):
        return rows_of(f, parity * unit, half)

    def second_half(f):
        return rows_of(f, parity * unit + half, half)

    y_hi, x = place.y_hi, place.x
    row = lambda y, step: place.row(y, x + step)
    own, near_left, near_right, far = (row(y_hi, k) for k in (0, 3, 1, 2))
    over, over_left, over_right, over_far = (row(1 - y_hi, k) for k in (0, 3, 1, 2))

    value_copies = [
        send(
            v_ref.at[:, at(place.fellow(k) * HEAD_SIZE, HEAD_SIZE)], vg_ref.at[mine], place.at_fellow(k)
        )
        for k in (1, 2, 3)
    ]
    from_left, from_right, from_over = pass_on(main(own), right, left, across)
    head_copies = []
    for k in (2, 3, 1):
        for src, dst in ((q_ref, qg_ref), (g_ref, gg_ref)):
            head_copies.append(
                send(
                    src.at[:, at(place.fellow(k) * width, width)],
                    dst.at[at(member * tokens, tokens)],
                    place.at_fellow(k),
                )
            )

    shares = {}
    crossing = {}

    def share(name, block):
        shares.setdefault(name, []).extend(pass_on(block, sibling))

    def cross(name, f):
        bridge = parity * 3 * unit
        crossing[name] = (
            pass_on(rows_of(f, bridge, unit // 2), z_up)
            + pass_on(rows_of(f, bridge + unit // 2, unit // 2), z_down)
        )

    def land(name, f):
        for copy in crossing[name]:
            copy.wait_recv()
        share(name, rows_of(f, (1 - parity) * 3 * unit, unit))

    def project(name, f):
        for copy in shares.get(name, ()):
            copy.wait_recv()

        @pl.loop(0, 2)
        def _(part):
            rows = at(f * shard + part * (shard // 2), shard // 2)
            projected[...] += jnp.dot(inputs[:, rows], full[rows, :], preferred_element_type=jnp.float32)

    load.wait()
    project("own", own)
    for copy in value_copies:
        copy.wait_recv()
    owns[2].wait()
    ring = Ring(place, sender, vg_ref, lambda z: z * 4 * tokens, 4 * tokens)
    ring.step()

    from_left.wait_recv()
    far_first = pass_on(first_half(near_left), right)[0]
    from_right.wait_recv()
    far_second = pass_on(second_half(near_right), left)[0]
    from_over.wait_recv()
    over_from_left, over_from_right = pass_on(main(over), right, left)
    for name, f in (("near_left", near_left), ("near_right", near_right), ("over", over)):
        share(name, main(f))
        cross(name, f)
    ring.step()
    far_first.wait_recv()
    over_far_first = pass_on(first_half(far), across)[0]
    far_second.wait_recv()
    over_far_second = pass_on(second_half(far), across)[0]
    share("far", main(far))
    cross("far", far)
    ring.step()
    for name, f in (("near_left", near_left), ("near_right", near_right), ("over", over)):
        land(name, f)
    project("near_left", near_left)
    project("near_right", near_right)
    land("far", far)
    ring.run()
    project("over", over)
    over_from_left.wait_recv()
    share("over_left", main(over_left))
    cross("over_left", over_left)
    over_from_right.wait_recv()
    share("over_right", main(over_right))
    cross("over_right", over_right)
    project("far", far)
    over_far_first.wait_recv()
    over_far_second.wait_recv()
    share("over_far", main(over_far))
    cross("over_far", over_far)
    land("over_left", over_left)
    land("over_right", over_right)
    project("over_left", over_left)
    project("over_right", over_right)
    land("over_far", over_far)
    project("over_far", over_far)
    store = pltpu.make_async_copy(full, full_ref, own_sems.at[0])
    store.start()

    low_rank = projected[:, kv_width : kv_width + rank].astype(jnp.bfloat16)
    low_ref[...] = low_rank
    for f in range(8):
        up_ref[:, f * (kv_width // 8) : (f + 1) * (kv_width // 8)] = full[
            f * shard : f * shard + rank, kv_width + rank :
        ]
    keys[...] = (
        projected[:, :kv_width]
        + ADAPTER_SCALE * jnp.dot(low_rank, up_ref[...], preferred_element_type=jnp.float32)
    ).astype(jnp.bfloat16)
    own_keys = pltpu.make_async_copy(keys.at[:, columns], kg_ref.at[mine], own_sems.at[4])
    own_keys.start()

    def exchange(device, fellow):
        return send(keys.at[:, at(fellow * HEAD_SIZE, HEAD_SIZE)], kg_ref.at[mine], device)

    to_sibling = exchange(sibling, member + 1 - 2 * place.core)
    other = [
        exchange(place.at_fellow(k), place.fellow(k)) for k in (2,)
    ]
    third = lax.rem(member + 3 - 2 * place.core, 4)
    other.append(exchange(place.of_context(place.z * 4 + third), third))
    rings = [
        Ring(place, sender, kg_ref, lambda z: (z * 4 + place.y_lo * 2) * tokens, 2 * tokens),
        Ring(place, sender, kg_ref, lambda z: (z * 4 + (1 - place.y_lo) * 2) * tokens, 2 * tokens),
    ]
    to_sibling.wait_recv()
    own_keys.wait()
    rings[0].step()
    for copy in other:
        copy.wait_recv()
    rings[1].step()
    while any(ring.flying for ring in rings):
        for ring in rings:
            ring.step()
    for copy in head_copies:
        copy.wait_recv()
    sender.finish()
    owns[0].wait()
    owns[1].wait()
    store.wait()


def attention_kernel(
    zs,
    list_ref,
    doc_smem,
    doc_ref,
    q_hbm,
    g_hbm,
    k_hbm,
    v_hbm,
    dq_hbm,
    dkv_hbm,
    queries,
    gradients,
    keys,
    values,
    totals,
    scores,
    grads,
    dq_rows,
    rounded,
    firsts,
    starts,
    load_sems,
    store_sems,
):
    to_exponent = math.log2(math.e) / math.sqrt(HEAD_SIZE)
    inv_root = 1.0 / math.sqrt(HEAD_SIZE)
    lanes = GROUPS * SPAN
    spans = list_ref.shape[0]
    own_spans = queries.shape[0] // SPAN
    z = lax.div(lax.axis_index("context"), 4)
    length = spans * SPAN

    loads = [
        pltpu.make_async_copy(q_hbm, queries, load_sems.at[0]),
        pltpu.make_async_copy(g_hbm, gradients, load_sems.at[1]),
    ]
    for load in loads:
        load.start()

    def span_copies(s):
        src, dst = at(s * SPAN, SPAN), at(list_ref[s] * SPAN, SPAN)
        return (
            pltpu.make_async_copy(k_hbm.at[src], keys.at[dst], load_sems.at[2]),
            pltpu.make_async_copy(v_hbm.at[src], values.at[dst], load_sems.at[3]),
        )

    @pl.loop(0, spans)
    def _(s):
        for load in span_copies(s):
            load.start()

    keys[length:, :] = jnp.zeros((KEY_TILE, HEAD_SIZE), jnp.bfloat16)
    values[length:, :] = jnp.zeros((KEY_TILE, HEAD_SIZE), jnp.bfloat16)

    @pl.loop(0, spans + KEY_TILE // SPAN)
    def _(n):
        totals[at(n * SPAN, SPAN), :] = jnp.zeros((SPAN, 2 * HEAD_SIZE), jnp.float32)

    def document_start(position):
        document = doc_smem[0, position]

        def narrow(_, carry):
            low, high = carry
            middle = lax.shift_right_logical(low + high, 1)
            earlier = doc_smem[0, middle] < document
            return jnp.where(earlier, middle + 1, low), jnp.where(earlier, high, middle)

        return lax.fori_loop(0, 12, narrow, (jnp.maximum(position - 1024, 0), position))[0]

    shape = (own_spans, 2 * SPAN)
    row = lax.broadcasted_iota(jnp.int32, shape, 0)
    lane = lax.broadcasted_iota(jnp.int32, shape, 1)
    row_begin, row_first = jnp.zeros(shape, jnp.int32), jnp.zeros(shape, jnp.int32)
    for i in range(own_spans):
        slot = list_ref[z * own_spans + i]
        begin = lax.shift_right_logical(slot, 1) * 2 * SPAN
        starts[i : i + 1, :] = doc_ref[0:1, pl.ds(pl.multiple_of(begin, 2 * SPAN), 2 * SPAN)]
        row_begin = jnp.where(row == i, begin, row_begin)
        row_first = jnp.where(row == i, document_start(begin), row_first)
        firsts[i] = lax.shift_right_logical(document_start(slot * SPAN), 6)
    documents = starts[...]
    changes = jnp.where((lane > 0) & (documents != pltpu.roll(documents, 1, 1)), lane, 0)
    for step in (1, 2, 4, 8, 16, 32, 64):
        changes = jnp.maximum(changes, jnp.where(lane >= step, pltpu.roll(changes, step, 1), 0))
    starts[...] = jnp.where(changes == 0, row_first, row_begin + changes)

    for load in loads:
        load.wait()

    pltpu.make_async_copy(k_hbm, keys.at[:length], load_sems.at[2]).wait()
    pltpu.make_async_copy(v_hbm, values.at[:length], load_sems.at[3]).wait()

    @pl.loop(0, own_spans)
    def _(i):
        slot, first = list_ref[z * own_spans + i], firsts[i]
        own = at(i * SPAN, SPAN)
        q_rows = jnp.concatenate(
            [queries[own, g * HEAD_SIZE : (g + 1) * HEAD_SIZE] for g in range(GROUPS)], axis=0
        )
        g_rows = jnp.concatenate(
            [gradients[own, g * HEAD_SIZE : (g + 1) * HEAD_SIZE] for g in range(GROUPS)], axis=0
        )
        pair = starts[pl.ds(i, 1), :]
        own_start = jnp.where(lax.rem(slot, 2) == 1, pair[:, SPAN:], pair[:, :SPAN])
        q_start = jnp.concatenate([own_start] * GROUPS, axis=1) - first * SPAN
        lane = lax.broadcasted_iota(jnp.int32, (1, lanes), 1)
        q_pos = (slot - first) * SPAN + lax.rem(lane, SPAN)
        tiles = lax.div(slot - first + KEY_TILE // SPAN, KEY_TILE // SPAN)

        def rows_at(t, first=first):
            return pl.ds(pl.multiple_of(first * SPAN + t * KEY_TILE, SPAN), KEY_TILE)

        def peak_step(t, peak, q_rows=q_rows, q_start=q_start, q_pos=q_pos, rows_at=rows_at):
            raw = lax.dot_general(
                keys[rows_at(t), :], q_rows, (((1,), (1,)), ((), ())), preferred_element_type=jnp.float32
            )
            key_pos = lax.broadcasted_iota(jnp.int32, (KEY_TILE, lanes), 0)
            raw = jnp.where(
                (key_pos >= q_start - t * KEY_TILE) & (key_pos <= q_pos - t * KEY_TILE), raw, NEGATIVE_FILL
            )
            scores[t] = raw
            grads[t] = lax.dot_general(
                values[rows_at(t), :], g_rows, (((1,), (1,)), ((), ())), preferred_element_type=jnp.float32
            )
            return jnp.maximum(peak, jnp.max(raw, axis=0, keepdims=True))

        peak = lax.fori_loop(0, tiles, peak_step, jnp.full((1, lanes), NEGATIVE_FILL, jnp.float32))

        def sum_step(t, carry, peak=peak):
            normalizer, weighted = carry
            weights = jnp.exp2((scores[t] - peak) * to_exponent)
            scores[t] = weights
            return (
                normalizer + jnp.sum(weights, axis=0, keepdims=True),
                weighted + jnp.sum(weights * grads[t], axis=0, keepdims=True),
            )

        zero = jnp.zeros((1, lanes), jnp.float32)
        normalizer, weighted = lax.fori_loop(0, tiles, sum_step, (zero, zero))
        inverse = 1.0 / normalizer
        row_terms = weighted * inverse

        def grad_step(t, dq, q_rows=q_rows, g_rows=g_rows, inverse=inverse, row_terms=row_terms, rows_at=rows_at):
            rows = rows_at(t)
            probability = scores[t] * inverse
            dscore = (probability * (grads[t] - row_terms) * inv_root).astype(jnp.bfloat16)
            prob_low = probability.astype(jnp.bfloat16)
            totals[rows, :HEAD_SIZE] += jnp.dot(dscore, q_rows, preferred_element_type=jnp.float32)
            totals[rows, HEAD_SIZE:] += jnp.dot(prob_low, g_rows, preferred_element_type=jnp.float32)
            return dq + lax.dot_general(
                keys[rows, :], dscore, (((0,), (0,)), ((), ())), preferred_element_type=jnp.float32
            )

        dq = lax.fori_loop(0, tiles, grad_step, jnp.zeros((HEAD_SIZE, lanes), jnp.float32))
        dq = dq.T.astype(jnp.bfloat16)
        for g in range(GROUPS):
            dq_rows[own, g * HEAD_SIZE : (g + 1) * HEAD_SIZE] = dq[g * SPAN : (g + 1) * SPAN]
        pltpu.make_async_copy(dq_rows.at[own], dq_hbm.at[own], store_sems.at[0]).start()

    @pl.loop(0, spans)
    def _(s):
        rows = at(s * SPAN, SPAN)
        rounded[rows, :] = totals[at(list_ref[s] * SPAN, SPAN), :].astype(jnp.bfloat16)
        pltpu.make_async_copy(rounded.at[rows], dkv_hbm.at[rows], store_sems.at[1]).start()

    pltpu.make_async_copy(dq_rows, dq_hbm, store_sems.at[0]).wait()
    pltpu.make_async_copy(rounded, dkv_hbm, store_sems.at[1]).wait()


REDUCE_CUTS = 2


def reduce_plan(zs):
    half = zs // 2
    return [(1, 0, half), (-1, 1, half), (-1, 0, half - 1), (1, 1, half - 1)]


def finish_kernel(
    zs,
    dkv_ref,
    dqg_ref,
    low_ref,
    up_ref,
    x_hbm,
    full_hbm,
    dq_ref,
    vg_ref,
    grad_ref,
    total_ref,
    out,
    held,
    done,
    key_grad,
    inputs,
    full,
    stacked,
    parts,
    pair_in,
    row,
    far_in,
    near_out,
    near_in,
    y_out,
    y_in,
    z_out,
    z_in,
    lo_out,
    lo_in,
    send_sems,
    recv_sems,
    own_sems,
):
    place = Place(zs)
    tokens = dq_ref.shape[0]
    width = GROUPS * HEAD_SIZE
    member = place.member
    rows = 4 * tokens
    cut = rows // REDUCE_CUTS
    loads = [
        pltpu.make_async_copy(x_hbm, inputs, own_sems.at[0]),
        pltpu.make_async_copy(full_hbm, full, own_sems.at[1]),
    ]
    for load in loads:
        load.start()
    own_query = pltpu.make_async_copy(
        dqg_ref.at[at(member * tokens, tokens)], dq_ref.at[:, at(member * width, width)], own_sems.at[2]
    )
    own_query.start()
    right, left, across = place.at_x(1), place.at_x(3), place.across_y()
    sibling, other_lo = place.sibling(), place.other_y_lo()
    greet(
        [place.at_fellow(k) for k in (1, 2, 3)]
        + [place.at_z(k) for k in range(1, zs)]
        + [right, left, across]
    )
    sender = Sender(send_sems, recv_sems)
    send = sender.send

    plan = reduce_plan(zs)
    last = {}
    slot = 0
    query_copies = []
    for step in range(zs // 2):
        for piece in range(REDUCE_CUTS):
            for chain, (direction, column, hops) in enumerate(plan):
                if step >= hops:
                    continue
                columns = slice(column * HEAD_SIZE, (column + 1) * HEAD_SIZE)
                destination = place.z_at(direction * (hops - step))
                mine = dkv_ref[at(destination * rows + piece * cut, cut), columns]
                if step > 0:
                    copy, before = last[chain, piece]
                    copy.wait_recv()
                    mine = (mine.astype(jnp.float32) + held[before].astype(jnp.float32)).astype(jnp.bfloat16)
                out[slot] = mine
                last[chain, piece] = (send(out.at[slot], held.at[slot], place.at_z(direction)), slot)
                slot += 1
        if step == 0:
            for k in (2, 3, 1):
                query_copies.append(
                    send(
                        dqg_ref.at[at(place.fellow(k) * tokens, tokens)],
                        dq_ref.at[:, at(member * width, width)],
                        place.at_fellow(k),
                    )
                )
    owns, key_copies, value_copies = [], [], []
    for column, target, copies in ((0, key_grad, key_copies), (1, vg_ref, value_copies)):
        columns = slice(column * HEAD_SIZE, (column + 1) * HEAD_SIZE)
        for piece in range(REDUCE_CUTS):
            total = dkv_ref[at(place.z * rows + piece * cut, cut), columns].astype(jnp.float32)
            for chain, (direction, its_column, hops) in enumerate(plan):
                if its_column == column and hops:
                    copy, before = last[chain, piece]
                    copy.wait_recv()
                    total = total + held[before].astype(jnp.float32)
            done[column, piece * cut : (piece + 1) * cut, :] = total.astype(jnp.bfloat16)
        landing = target.at[:, at(member * HEAD_SIZE, HEAD_SIZE)]
        own = pltpu.make_async_copy(
            done.at[column, at(member * tokens, tokens)], landing, own_sems.at[3 + column]
        )
        own.start()
        owns.append(own)
        for k in (2, 3, 1):
            copies.append(
                send(done.at[column, at(place.fellow(k) * tokens, tokens)], landing, place.at_fellow(k))
            )
    loads[0].wait()
    owns[0].wait()
    for copy in key_copies:
        copy.wait_recv()

    kg = key_grad[...]
    lifted = lax.dot_general(
        kg, up_ref[...], (((1,), (1,)), ((), ())), preferred_element_type=jnp.float32
    ).astype(jnp.bfloat16)
    scaled = (lifted.astype(jnp.float32) * ADAPTER_SCALE).astype(jnp.bfloat16)
    rank = lifted.shape[1]
    ranks = rank // 2
    kv_width = kg.shape[1]
    stacked[:, :kv_width] = kg
    stacked[:, kv_width:] = jnp.concatenate([scaled, jnp.zeros_like(scaled)], axis=1)
    up_part = (
        ADAPTER_SCALE
        * lax.dot_general(low_ref[...], kg, (((0,), (0,)), ((), ())), preferred_element_type=jnp.float32)
    ).astype(jnp.bfloat16)
    lanes = parts.shape[3] - 128
    share = kv_width // 8
    padding = jnp.zeros((rank, 128 - share), jnp.bfloat16)
    for f in range(8):
        block = jnp.concatenate([up_part[:, f * share : (f + 1) * share], padding], axis=1)
        parts[f, 0, :, lanes:] = block[:ranks]
        parts[f, 1, :, lanes:] = block[ranks:]

    @pl.loop(0, 8)
    def _(f):
        block = lax.dot_general(
            scaled, inputs[:, at(f * lanes, lanes)], (((0,), (0,)), ((), ())), preferred_element_type=jnp.float32
        ).astype(jnp.bfloat16)
        parts[f, 0, :, :lanes] = block[:ranks]
        parts[f, 1, :, :lanes] = block[ranks:]

    pair_copy = send(parts.at[:, 1 - place.core], pair_in, sibling)
    loads[1].wait()

    def input_gradient(begin, end):
        @pl.loop(begin, end)
        def _(j):
            some = at(j * lanes, lanes)
            grad_ref[:, some] = lax.dot_general(
                stacked[...], full[some, :], (((1,), (1,)), ((), ())), preferred_element_type=jnp.float32
            ).astype(jnp.bfloat16)

    input_gradient(0, 2)
    pair_copy.wait_recv()

    def add(*terms):
        total = terms[0].astype(jnp.float32)
        for term in terms[1:]:
            total = total + term.astype(jnp.float32)
        return total

    @pl.loop(0, 8)
    def _(f):
        row[f] = add(parts[f, pl.ds(place.core, 1)][0], pair_in[f]).astype(jnp.bfloat16)

    here = lambda y_hi, step: place.row(y_hi, place.x + step)
    far_copies = [
        send(row.at[here(0, 2)], far_in.at[0], right),
        send(row.at[here(1, 2)], far_in.at[1], left),
    ]
    near_copies = [
        send(row.at[here(1, 1)], near_in.at[0, 1], right),
        send(row.at[here(0, 3)], near_in.at[1, 0], left),
    ]
    input_gradient(2, 3)
    for way, (y_hi, step, device) in enumerate(((0, 1, right), (1, 3, left))):
        far_copies[way].wait_recv()
        near_out[way] = add(row[here(y_hi, step)], far_in[way]).astype(jnp.bfloat16)
        near_copies.append(send(near_out.at[way], near_in.at[way, y_hi], device))
    input_gradient(3, 5)
    for copy in near_copies:
        copy.wait_recv()

    def over_x(y_hi):
        return add(row[here(y_hi, 0)], near_in[0, y_hi], near_in[1, y_hi])

    y_out[...] = over_x(1 - place.y_hi).astype(jnp.bfloat16)
    y_copy = send(y_out, y_in, across)
    mine = over_x(place.y_hi)
    input_gradient(5, 6)
    y_copy.wait_recv()
    mine = add(mine, y_in[...])
    chunk_lanes = lanes // zs
    cuts = min(zs, 4)
    small = ranks // cuts
    for j in range(zs):
        z_out[j, :ranks] = mine[:, j * chunk_lanes : (j + 1) * chunk_lanes]
        z_out[j, ranks:] = mine[(j % cuts) * small : (j % cuts + 1) * small, lanes:]
    z_copies = []
    for k in sorted(range(1, zs), key=lambda k: -min(k, zs - k)):
        z_copies.append(send(z_out.at[place.z_at(k)], z_in.at[k - 1], place.at_z(k)))
    input_gradient(6, 7)
    for copy in z_copies:
        copy.wait_recv()
    chunk = z_out[place.z]
    for k in range(zs - 1):
        chunk = chunk + z_in[k]
    lo_out[...] = chunk
    lo_copy = send(lo_out, lo_in, other_lo)
    lo_copy.wait_recv()
    chunk = chunk + lo_in[...]
    total_ref[pl.ds(place.core, 1), pl.ds(place.z, 1)] = chunk[None, None]
    block = total_ref.at[place.core, place.z]
    z_copies = []
    for k in sorted(range(1, zs), key=lambda k: -min(k, zs - k)):
        z_copies.append(send(block, block, place.at_z(k)))
    input_gradient(7, 8)
    for copy in z_copies:
        copy.wait_recv()
    block = total_ref.at[place.core]
    send(block, block, sibling).wait_recv()
    for copy in value_copies + query_copies:
        copy.wait_recv()
    sender.finish()
    owns[1].wait()
    own_query.wait()


def dma(count):
    return pltpu.SemaphoreType.DMA((count,))


def params(collective_id=None):
    if collective_id is None:
        return pltpu.CompilerParams(vmem_limit_bytes=56 << 20)
    return pltpu.CompilerParams(
        vmem_limit_bytes=48 << 20, collective_id=collective_id, has_side_effects=True
    )


def body(
    zs,
    inputs,
    queries,
    values,
    output_gradient,
    key_base_weight,
    adapter_down,
    adapter_up,
    span_slot_index,
    segment_document,
):
    bf16, f32, i32 = jnp.bfloat16, jnp.float32, jnp.int32
    rows_in = inputs[0]
    tokens, model = rows_in.shape
    shard, kv_width = key_base_weight.shape
    rank = adapter_down.shape[1]
    length = segment_document.shape[1]
    width = GROUPS * HEAD_SIZE
    half = zs // 2
    shape = jax.ShapeDtypeStruct
    packed_width = kv_width + rank + adapter_up.shape[1]

    copies = 3 + 3 + 6 + 2 + 2 + 2 + 7 * 4 + 3 + 3 * 2 * half
    full, query_group, gradient_group, value_all, key_all, low_rank, complete_up = pl.pallas_call(
        functools.partial(keys_kernel, zs),
        out_shape=(
            shape((model, packed_width), bf16),
            shape((4 * tokens, width), bf16),
            shape((4 * tokens, width), bf16),
            shape((length, HEAD_SIZE), bf16),
            shape((length, HEAD_SIZE), bf16),
            shape((tokens, rank), bf16),
            shape((rank, kv_width), bf16),
        ),
        in_specs=[VMEM] * 3 + [ANY] * 4,
        out_specs=(ANY,) * 5 + (VMEM,) * 2,
        scratch_shapes=[
            pltpu.VMEM((model, packed_width), bf16),
            pltpu.VMEM((tokens, model), bf16),
            pltpu.VMEM((tokens, packed_width), f32),
            pltpu.VMEM((tokens, kv_width), bf16),
            dma(copies),
            dma(copies),
            dma(5),
        ],
        compiler_params=params(0),
        name="gather_weights_and_keys",
    )(
        key_base_weight,
        adapter_down,
        adapter_up,
        rows_in,
        queries[0],
        output_gradient[0],
        values[0],
    )

    span_rows = 4 * tokens
    tile_rows = (1024 // KEY_TILE + 1, KEY_TILE, GROUPS * SPAN)
    query_grad_group, partial_sums = pl.pallas_call(
        functools.partial(attention_kernel, zs),
        out_shape=(
            jax.ShapeDtypeStruct((span_rows, width), bf16),
            jax.ShapeDtypeStruct((length, 2 * HEAD_SIZE), bf16),
        ),
        in_specs=[SMEM, SMEM, VMEM] + [ANY] * 4,
        out_specs=(ANY, ANY),
        scratch_shapes=[
            pltpu.VMEM((span_rows, width), bf16),
            pltpu.VMEM((span_rows, width), bf16),
            pltpu.VMEM((length + KEY_TILE, HEAD_SIZE), bf16),
            pltpu.VMEM((length + KEY_TILE, HEAD_SIZE), bf16),
            pltpu.VMEM((length + KEY_TILE, 2 * HEAD_SIZE), f32),
            pltpu.VMEM(tile_rows, f32),
            pltpu.VMEM(tile_rows, f32),
            pltpu.VMEM((span_rows, width), bf16),
            pltpu.VMEM((length, 2 * HEAD_SIZE), bf16),
            pltpu.SMEM((span_rows // SPAN,), i32),
            pltpu.VMEM((span_rows // SPAN, 2 * SPAN), i32),
            dma(4),
            dma(2),
        ],
        compiler_params=params(),
        name="attention_gradients",
    )(
        span_slot_index[0],
        segment_document,
        segment_document,
        query_group,
        gradient_group,
        key_all,
        value_all,
    )

    hops = REDUCE_CUTS * sum(hops for _, _, hops in reduce_plan(zs))
    cut = 4 * tokens // REDUCE_CUTS
    ranks = rank // 2
    lanes = shard + 128
    chunk = (ranks + ranks // min(zs, 4), shard // zs)
    copies = hops + 9 + 1 + 6 + 1 + 2 * (zs - 1) + 2
    query_grad, value_grad, input_gradient, totals = pl.pallas_call(
        functools.partial(finish_kernel, zs),
        out_shape=(
            shape((tokens, QUERY_HEADS * HEAD_SIZE), bf16),
            shape((tokens, kv_width), bf16),
            shape((tokens, model), bf16),
            shape((2, zs) + chunk, f32),
        ),
        in_specs=[VMEM, ANY, VMEM, VMEM, ANY, ANY],
        out_specs=(ANY, ANY, VMEM, VMEM),
        scratch_shapes=[
            pltpu.VMEM((hops, cut, HEAD_SIZE), bf16),
            pltpu.VMEM((hops, cut, HEAD_SIZE), bf16),
            pltpu.VMEM((2, 4 * tokens, HEAD_SIZE), bf16),
            pltpu.VMEM((tokens, kv_width), bf16),
            pltpu.VMEM((tokens, model), bf16),
            pltpu.VMEM((model, packed_width), bf16),
            pltpu.VMEM((tokens, packed_width), bf16),
            pltpu.VMEM((8, 2, ranks, lanes), bf16),
            pltpu.VMEM((8, ranks, lanes), bf16),
            pltpu.VMEM((8, ranks, lanes), bf16),
            pltpu.VMEM((2, ranks, lanes), bf16),
            pltpu.VMEM((2, ranks, lanes), bf16),
            pltpu.VMEM((2, 2, ranks, lanes), bf16),
            pltpu.VMEM((ranks, lanes), bf16),
            pltpu.VMEM((ranks, lanes), bf16),
            pltpu.VMEM((zs,) + chunk, f32),
            pltpu.VMEM((zs - 1,) + chunk, f32),
            pltpu.VMEM(chunk, f32),
            pltpu.VMEM(chunk, f32),
            dma(copies),
            dma(copies),
            dma(5),
        ],
        compiler_params=params(1),
        name="sum_gradients",
    )(partial_sums, query_grad_group, low_rank, complete_up, rows_in, full)

    share = kv_width // 8
    down_share = totals[:, :, :ranks].transpose(1, 3, 0, 2).reshape(shard, rank)
    up_share = totals[:, : min(zs, 4), ranks:, :share].reshape(rank, share)
    return (query_grad[None], value_grad[None], input_gradient[None], down_share, up_share)


def solution(mesh):
    spread, rows = P("fsdp", "context", None), P("fsdp", None)
    placed = (spread, spread, spread, spread, rows, rows, P(None, "fsdp"), rows, rows)
    return jax.shard_map(
        functools.partial(body, mesh.shape["context"] // 4),
        mesh=mesh,
        in_specs=placed,
        out_specs=(spread, spread, spread, rows, P(None, "fsdp")),
        check_vma=False,
    )
```

```python
import functools
import math

import jax
import jax.numpy as jnp
from jax import lax
from jax.experimental import pallas as pl
from jax.experimental.pallas import tpu as pltpu
from jax.sharding import PartitionSpec as P

QUERY_HEADS = 32
KEY_VALUE_HEADS = 4
HEAD_SIZE = 128
GROUPS = QUERY_HEADS // KEY_VALUE_HEADS
SPAN = 64
ADAPTER_SCALE = 0.5
NEGATIVE_FILL = -1e30
KEY_TILE = 256
MESH = pl.DeviceIdType.MESH
ANY = pl.BlockSpec(memory_space=pl.ANY)
VMEM = pl.BlockSpec(memory_space=pltpu.VMEM)
HBM = pl.BlockSpec(memory_space=pltpu.HBM)
SMEM = pl.BlockSpec(memory_space=pltpu.SMEM)


def at(start, size):
    return pl.ds(pl.multiple_of(start, size), size)


class Place:
    def __init__(self, zs):
        self.zs = zs
        self.fsdp = lax.axis_index("fsdp")
        self.context = lax.axis_index("context")
        self.y_hi, self.x = lax.div(self.fsdp, 4), lax.rem(self.fsdp, 4)
        self.z, self.member = lax.div(self.context, 4), lax.rem(self.context, 4)
        self.y_lo, self.core = lax.div(self.member, 2), lax.rem(self.member, 2)

    def row(self, y_hi, x):
        return y_hi * 4 + lax.rem(x, 4)

    def at_x(self, step):
        return {"fsdp": self.row(self.y_hi, self.x + step), "context": self.context}

    def across_y(self):
        return {
            "fsdp": self.row(1 - self.y_hi, self.x),
            "context": self.z * 4 + (1 - self.y_lo) * 2 + self.core,
        }

    def other_y_lo(self):
        return self.of_context(self.z * 4 + (1 - self.y_lo) * 2 + self.core)

    def sibling(self):
        return self.of_context(self.z * 4 + self.y_lo * 2 + 1 - self.core)

    def of_context(self, context):
        return {"fsdp": self.fsdp, "context": context}

    def fellow(self, k):
        return lax.rem(self.member + k, 4)

    def at_fellow(self, k):
        return self.of_context(self.z * 4 + self.fellow(k))

    def z_at(self, step):
        return lax.rem(self.z + step + self.zs, self.zs)

    def at_z(self, step):
        return self.of_context(self.z_at(step) * 4 + self.member)


def greet(partners):
    barrier = pltpu.get_barrier_semaphore()
    for partner in partners:
        pl.semaphore_signal(barrier, inc=1, device_id=partner, device_id_type=MESH)
    pl.semaphore_wait(barrier, len(partners))


class Sender:
    def __init__(self, send_sems, recv_sems):
        self.send_sems, self.recv_sems, self.copies = send_sems, recv_sems, []

    def send(self, src, dst, device):
        k = len(self.copies)
        assert k < self.send_sems.shape[0]
        copy = pltpu.make_async_remote_copy(
            src_ref=src,
            dst_ref=dst,
            send_sem=self.send_sems.at[k],
            recv_sem=self.recv_sems.at[k],
            device_id=device,
            device_id_type=MESH,
        )
        copy.start()
        self.copies.append(copy)
        return copy

    def finish(self):
        for copy in self.copies:
            copy.wait_send()


class Ring:
    def __init__(self, place, sender, buffer, block, rows):
        self.place, self.sender, self.buffer = place, sender, buffer
        self.block, self.rows, self.stage, self.flying = block, rows, 0, ()
        self.stages = place.zs // 2

    def step(self):
        for copy in self.flying:
            copy.wait_recv()
        self.flying = ()
        if self.stage == self.stages:
            return
        right_at, left_at = self.block(self.place.z_at(-self.stage)), self.block(self.place.z_at(self.stage))
        if self.stage < self.stages - 1:
            right_rows, left_rows = at(right_at, self.rows), at(left_at, self.rows)
        else:
            cut = self.rows // 2
            right_rows, left_rows = at(right_at, cut), at(left_at + cut, cut)
        buffer, send = self.buffer, self.sender.send
        self.flying = (
            send(buffer.at[right_rows], buffer.at[right_rows], self.place.at_z(1)),
            send(buffer.at[left_rows], buffer.at[left_rows], self.place.at_z(-1)),
        )
        self.stage += 1

    def run(self):
        while self.stage < self.stages or self.flying:
            self.step()


def keys_kernel(
    zs,
    w_hbm,
    d_ref,
    u_ref,
    x_hbm,
    q_ref,
    g_ref,
    v_ref,
    full_ref,
    qg_ref,
    gg_ref,
    vg_ref,
    kg_ref,
    low_ref,
    up_ref,
    full,
    inputs,
    projected,
    pair_in,
    keys,
    send_sems,
    recv_sems,
    own_sems,
):
    place = Place(zs)
    tokens = q_ref.shape[0]
    shard, kv_width = w_hbm.shape
    rank = d_ref.shape[0]
    unit = shard // 8
    width = GROUPS * HEAD_SIZE
    member = place.member
    mine = at((place.z * 4 + member) * tokens, tokens)
    columns = at(member * HEAD_SIZE, HEAD_SIZE)
    piece = shard // 2

    def columns_of(f, core):
        return at(f * shard + core * piece, piece)

    def own_inputs(f):
        return pltpu.make_async_copy(
            x_hbm.at[:, columns_of(f, place.core)],
            inputs.at[:tokens, f * piece : (f + 1) * piece],
            own_sems.at[0],
        )

    for f in range(8):
        own_inputs(f).start()
    owns = [
        pltpu.make_async_copy(
            q_ref.at[:, at(member * width, width)], qg_ref.at[at(member * tokens, tokens)], own_sems.at[1]
        ),
        pltpu.make_async_copy(
            g_ref.at[:, at(member * width, width)], gg_ref.at[at(member * tokens, tokens)], own_sems.at[2]
        ),
        pltpu.make_async_copy(v_ref.at[:, columns], vg_ref.at[mine], own_sems.at[3]),
    ]
    for own in owns:
        own.start()
    own_rows = at(place.fsdp * shard, shard)
    weights = pltpu.make_async_copy(w_hbm, full.at[own_rows, :kv_width], own_sems.at[5])
    weights.start()
    filler = jnp.zeros((shard // 2 - rank, u_ref.shape[1]), jnp.bfloat16)
    up_rows = jnp.concatenate([u_ref[...], filler] * 2, axis=0)
    full[own_rows, kv_width:] = jnp.concatenate([d_ref[...].T, up_rows], axis=1)
    projected[...] = jnp.zeros_like(projected)
    weights.wait()

    right, left, across, sibling = place.at_x(1), place.at_x(3), place.across_y(), place.sibling()
    z_up, z_down = place.at_z(1), place.at_z(-1)
    greet([right, left, across] + [place.at_fellow(k) for k in (1, 2, 3)] + [z_up, z_down])
    sender = Sender(send_sems, recv_sems)
    send = sender.send

    parity = lax.rem(place.z, 2)

    def rows_of(f, offset, size):
        begin = f * shard + place.core * 4 * unit + offset
        return full.at[pl.ds(pl.multiple_of(begin, unit // 2), size)]

    def bridge(f):
        return rows_of(f, parity * 3 * unit, unit)

    def body(f):
        return rows_of(f, unit, 2 * unit)

    def low_body(f):
        return rows_of(f, unit, unit // 2)

    def high_body(f):
        return rows_of(f, unit + unit // 2, 3 * unit // 2)

    def pass_on(block, *devices):
        return [send(block, block, device) for device in devices]

    y_hi, x = place.y_hi, place.x
    row = lambda y, step: place.row(y, x + step)
    own, near_left, near_right, far = (row(y_hi, k) for k in (0, 3, 1, 2))
    over, over_left, over_right, over_far = (row(1 - y_hi, k) for k in (0, 3, 1, 2))

    sibling_inputs = [
        send(
            x_hbm.at[:, columns_of(f, 1 - place.core)],
            inputs.at[tokens:, f * piece : (f + 1) * piece],
            sibling,
        )
        for f in range(8)
    ]
    value_copies = [
        send(
            v_ref.at[:, at(place.fellow(k) * HEAD_SIZE, HEAD_SIZE)], vg_ref.at[mine], place.at_fellow(k)
        )
        for k in (1, 2, 3)
    ]
    near_left_bridge, near_right_bridge, over_bridge = pass_on(bridge(own), right, left, across)
    near_left_body, near_right_body, over_body = pass_on(body(own), right, left, across)
    shares = {}
    crossing = {}

    def share(name, f):
        shares[name] = pass_on(rows_of(f, parity * unit, 3 * unit), sibling)[0]

    def cross(name, f):
        begin = parity * 3 * unit
        crossing[name] = (
            pass_on(rows_of(f, begin, unit // 2), z_up)
            + pass_on(rows_of(f, begin + unit // 2, unit // 2), z_down)
        )

    def land(name, f):
        for copy in crossing[name]:
            copy.wait_recv()
        shares[name, "rest"] = pass_on(rows_of(f, (1 - parity) * 3 * unit, unit), sibling)[0]

    def multiply(f, offset, size):
        columns = pl.ds(pl.multiple_of(f * piece + offset, unit), size)
        projected[...] += jnp.dot(
            inputs[:, columns], rows_of(f, offset, size)[...], preferred_element_type=jnp.float32
        )

    def project(f):
        multiply(f, parity * unit, 3 * unit)

    def project_rest(f):
        multiply(f, (1 - parity) * 3 * unit, unit)

    pltpu.make_async_copy(x_hbm.at[:, : 8 * piece], inputs.at[:tokens], own_sems.at[0]).wait()
    for copy in sibling_inputs:
        copy.wait_recv()
    multiply(own, 0, 4 * unit)

    near_left_bridge.wait_recv()
    far_bridge = pass_on(bridge(near_left), right)[0]
    cross("near_left", near_left)
    near_right_bridge.wait_recv()
    cross("near_right", near_right)
    over_bridge.wait_recv()
    over_left_bridge, over_right_bridge = pass_on(bridge(over), right, left)
    cross("over", over)
    head_copies = []
    for k in (2, 3, 1):
        for src, dst in ((q_ref, qg_ref), (g_ref, gg_ref)):
            head_copies.append(
                send(
                    src.at[:, at(place.fellow(k) * width, width)],
                    dst.at[at(member * tokens, tokens)],
                    place.at_fellow(k),
                )
            )

    near_left_body.wait_recv()
    far_low = pass_on(low_body(near_left), right)[0]
    near_right_body.wait_recv()
    far_high = pass_on(high_body(near_right), left)[0]
    over_body.wait_recv()
    over_left_body, over_right_body = pass_on(body(over), right, left)
    share("near_left", near_left)
    share("near_right", near_right)
    share("over", over)
    far_bridge.wait_recv()
    over_far_bridge = pass_on(bridge(far), across)[0]
    cross("far", far)
    far_low.wait_recv()
    over_far_low = pass_on(low_body(far), across)[0]
    for name, f in (("near_left", near_left), ("near_right", near_right), ("over", over)):
        land(name, f)
    far_high.wait_recv()
    over_far_high = pass_on(high_body(far), across)[0]
    share("far", far)
    for copy in value_copies:
        copy.wait_recv()
    owns[2].wait()
    ring = Ring(place, sender, vg_ref, lambda z: z * 4 * tokens, 4 * tokens)
    over_left_bridge.wait_recv()
    cross("over_left", over_left)
    over_right_bridge.wait_recv()
    cross("over_right", over_right)
    over_far_bridge.wait_recv()
    cross("over_far", over_far)
    land("far", far)
    for f in (near_left, near_right, over, far):
        project(f)
        project_rest(f)
    over_left_body.wait_recv()
    project(over_left)
    share("over_left", over_left)
    over_right_body.wait_recv()
    project(over_right)
    share("over_right", over_right)
    for name, f in (("over_left", over_left), ("over_right", over_right), ("over_far", over_far)):
        land(name, f)
        project_rest(f)
    over_far_low.wait_recv()
    over_far_high.wait_recv()
    project(over_far)
    pair_copy = send(projected.at[tokens:], pair_in, sibling)
    share("over_far", over_far)

    def stores(core):
        for f in range(8):
            rows = columns_of(f, core)
            pltpu.make_async_copy(full.at[rows], full_ref.at[rows], own_sems.at[0]).start()

    stores(place.core)
    pair_copy.wait_recv()
    projection = projected[:tokens] + pair_in[...]

    low_rank = projection[:, kv_width : kv_width + rank].astype(jnp.bfloat16)
    low_ref[...] = low_rank
    for f in range(8):
        up_ref[:, f * (kv_width // 8) : (f + 1) * (kv_width // 8)] = full[
            at(f * shard + place.core * piece, rank), kv_width + rank :
        ]
    keys[...] = (
        projection[:, :kv_width]
        + ADAPTER_SCALE * jnp.dot(low_rank, up_ref[...], preferred_element_type=jnp.float32)
    ).astype(jnp.bfloat16)
    own_keys = pltpu.make_async_copy(keys.at[:, columns], kg_ref.at[mine], own_sems.at[4])
    own_keys.start()

    def exchange(device, fellow):
        return send(keys.at[:, at(fellow * HEAD_SIZE, HEAD_SIZE)], kg_ref.at[mine], device)

    to_sibling = exchange(sibling, member + 1 - 2 * place.core)
    other = [
        exchange(place.at_fellow(k), place.fellow(k)) for k in (2,)
    ]
    third = lax.rem(member + 3 - 2 * place.core, 4)
    other.append(exchange(place.of_context(place.z * 4 + third), third))
    rings = [
        Ring(place, sender, kg_ref, lambda z: (z * 4 + place.y_lo * 2) * tokens, 2 * tokens),
        Ring(place, sender, kg_ref, lambda z: (z * 4 + (1 - place.y_lo) * 2) * tokens, 2 * tokens),
    ]
    to_sibling.wait_recv()
    own_keys.wait()
    rings[0].step()
    for copy in other:
        copy.wait_recv()
    rings[1].step()
    for copy in shares.values():
        copy.wait_recv()
    stores(1 - place.core)
    rings.append(ring)
    ring.step()
    while any(some.flying for some in rings):
        for some in rings:
            some.step()
    for copy in head_copies:
        copy.wait_recv()
    sender.finish()
    owns[0].wait()
    owns[1].wait()
    pltpu.make_async_copy(full, full_ref, own_sems.at[0]).wait()


def attention_kernel(
    zs,
    list_ref,
    doc_smem,
    doc_ref,
    queries,
    gradients,
    k_ref,
    v_ref,
    dq_hbm,
    dkv_ref,
    keys,
    values,
    totals,
    scores,
    grads,
    dq_rows,
    firsts,
    starts,
    store_sem,
):
    to_exponent = math.log2(math.e) / math.sqrt(HEAD_SIZE)
    inv_root = 1.0 / math.sqrt(HEAD_SIZE)
    lanes = GROUPS * SPAN
    spans = list_ref.shape[0]
    own_spans = queries.shape[0] // SPAN
    z = lax.div(lax.axis_index("context"), 4)
    length = spans * SPAN

    keys[length:, :] = jnp.zeros((KEY_TILE, HEAD_SIZE), jnp.bfloat16)
    values[length:, :] = jnp.zeros((KEY_TILE, HEAD_SIZE), jnp.bfloat16)

    @pl.loop(0, spans + KEY_TILE // SPAN)
    def _(n):
        totals[at(n * SPAN, SPAN), :] = jnp.zeros((SPAN, 2 * HEAD_SIZE), jnp.float32)

    def document_start(position):
        document = doc_smem[0, position]

        def narrow(_, carry):
            low, high = carry
            middle = lax.shift_right_logical(low + high, 1)
            earlier = doc_smem[0, middle] < document
            return jnp.where(earlier, middle + 1, low), jnp.where(earlier, high, middle)

        return lax.fori_loop(0, 12, narrow, (jnp.maximum(position - 1024, 0), position))[0]

    shape = (own_spans, 2 * SPAN)
    row = lax.broadcasted_iota(jnp.int32, shape, 0)
    lane = lax.broadcasted_iota(jnp.int32, shape, 1)
    row_begin, row_first = jnp.zeros(shape, jnp.int32), jnp.zeros(shape, jnp.int32)
    for i in range(own_spans):
        slot = list_ref[z * own_spans + i]
        begin = lax.shift_right_logical(slot, 1) * 2 * SPAN
        starts[i : i + 1, :] = doc_ref[0:1, pl.ds(pl.multiple_of(begin, 2 * SPAN), 2 * SPAN)]
        row_begin = jnp.where(row == i, begin, row_begin)
        row_first = jnp.where(row == i, document_start(begin), row_first)
        firsts[i] = lax.shift_right_logical(document_start(slot * SPAN), 6)
    documents = starts[...]
    changes = jnp.where((lane > 0) & (documents != pltpu.roll(documents, 1, 1)), lane, 0)
    for step in (1, 2, 4, 8, 16, 32, 64):
        changes = jnp.maximum(changes, jnp.where(lane >= step, pltpu.roll(changes, step, 1), 0))
    starts[...] = jnp.where(changes == 0, row_first, row_begin + changes)

    @pl.loop(0, spans)
    def _(s):
        src, dst = at(s * SPAN, SPAN), at(list_ref[s] * SPAN, SPAN)
        keys[dst, :] = k_ref[src, :]
        values[dst, :] = v_ref[src, :]

    @pl.loop(0, own_spans)
    def _(i):
        slot, first = list_ref[z * own_spans + i], firsts[i]
        own = at(i * SPAN, SPAN)
        q_rows = jnp.concatenate(
            [queries[own, g * HEAD_SIZE : (g + 1) * HEAD_SIZE] for g in range(GROUPS)], axis=0
        )
        g_rows = jnp.concatenate(
            [gradients[own, g * HEAD_SIZE : (g + 1) * HEAD_SIZE] for g in range(GROUPS)], axis=0
        )
        pair = starts[pl.ds(i, 1), :]
        own_start = jnp.where(lax.rem(slot, 2) == 1, pair[:, SPAN:], pair[:, :SPAN])
        q_start = jnp.concatenate([own_start] * GROUPS, axis=1) - first * SPAN
        lane = lax.broadcasted_iota(jnp.int32, (1, lanes), 1)
        q_pos = (slot - first) * SPAN + lax.rem(lane, SPAN)
        tiles = lax.div(slot - first + KEY_TILE // SPAN, KEY_TILE // SPAN)

        def rows_at(t, first=first):
            return pl.ds(pl.multiple_of(first * SPAN + t * KEY_TILE, SPAN), KEY_TILE)

        def peak_step(t, peak, q_rows=q_rows, q_start=q_start, q_pos=q_pos, rows_at=rows_at):
            raw = lax.dot_general(
                keys[rows_at(t), :], q_rows, (((1,), (1,)), ((), ())), preferred_element_type=jnp.float32
            )
            key_pos = lax.broadcasted_iota(jnp.int32, (KEY_TILE, lanes), 0)
            raw = jnp.where(
                (key_pos >= q_start - t * KEY_TILE) & (key_pos <= q_pos - t * KEY_TILE), raw, NEGATIVE_FILL
            )
            scores[t] = raw
            grads[t] = lax.dot_general(
                values[rows_at(t), :], g_rows, (((1,), (1,)), ((), ())), preferred_element_type=jnp.float32
            )
            return jnp.maximum(peak, jnp.max(raw, axis=0, keepdims=True))

        peak = lax.fori_loop(0, tiles, peak_step, jnp.full((1, lanes), NEGATIVE_FILL, jnp.float32))

        def sum_step(t, carry, peak=peak):
            normalizer, weighted = carry
            weights = jnp.exp2((scores[t] - peak) * to_exponent)
            scores[t] = weights
            return (
                normalizer + jnp.sum(weights, axis=0, keepdims=True),
                weighted + jnp.sum(weights * grads[t], axis=0, keepdims=True),
            )

        zero = jnp.zeros((1, lanes), jnp.float32)
        normalizer, weighted = lax.fori_loop(0, tiles, sum_step, (zero, zero))
        inverse = 1.0 / normalizer
        row_terms = weighted * inverse

        def grad_step(t, dq, q_rows=q_rows, g_rows=g_rows, inverse=inverse, row_terms=row_terms, rows_at=rows_at):
            rows = rows_at(t)
            probability = scores[t] * inverse
            dscore = (probability * (grads[t] - row_terms) * inv_root).astype(jnp.bfloat16)
            prob_low = probability.astype(jnp.bfloat16)
            totals[rows, :HEAD_SIZE] += jnp.dot(dscore, q_rows, preferred_element_type=jnp.float32)
            totals[rows, HEAD_SIZE:] += jnp.dot(prob_low, g_rows, preferred_element_type=jnp.float32)
            return dq + lax.dot_general(
                keys[rows, :], dscore, (((0,), (0,)), ((), ())), preferred_element_type=jnp.float32
            )

        dq = lax.fori_loop(0, tiles, grad_step, jnp.zeros((HEAD_SIZE, lanes), jnp.float32))
        dq = dq.T.astype(jnp.bfloat16)
        for g in range(GROUPS):
            dq_rows[own, g * HEAD_SIZE : (g + 1) * HEAD_SIZE] = dq[g * SPAN : (g + 1) * SPAN]
        pltpu.make_async_copy(dq_rows.at[own], dq_hbm.at[own], store_sem).start()

    @pl.loop(0, spans)
    def _(s):
        dkv_ref[at(s * SPAN, SPAN), :] = totals[at(list_ref[s] * SPAN, SPAN), :].astype(jnp.bfloat16)

    pltpu.make_async_copy(dq_rows, dq_hbm, store_sem).wait()


REDUCE_CUTS = 2


def reduce_plan(zs):
    half = zs // 2
    return [(1, 0, half), (-1, 1, half), (-1, 0, half - 1), (1, 1, half - 1)]


def finish_kernel(
    zs,
    dkv_ref,
    dqg_ref,
    low_ref,
    up_ref,
    x_hbm,
    full_hbm,
    dq_ref,
    vg_ref,
    grad_ref,
    down_ref,
    up_out,
    total_ref,
    out,
    held,
    done,
    key_grad,
    inputs,
    full,
    stacked,
    parts,
    pair_in,
    row,
    far_in,
    near_out,
    near_in,
    y_out,
    y_in,
    z_out,
    z_in,
    lo_out,
    lo_in,
    send_sems,
    recv_sems,
    own_sems,
):
    place = Place(zs)
    tokens = dq_ref.shape[0]
    width = GROUPS * HEAD_SIZE
    member = place.member
    rows = 4 * tokens
    cut = rows // REDUCE_CUTS
    loads = [
        pltpu.make_async_copy(x_hbm, inputs, own_sems.at[0]),
        pltpu.make_async_copy(full_hbm, full, own_sems.at[1]),
    ]
    for load in loads:
        load.start()
    own_query = pltpu.make_async_copy(
        dqg_ref.at[at(member * tokens, tokens)], dq_ref.at[:, at(member * width, width)], own_sems.at[2]
    )
    own_query.start()
    right, left, across = place.at_x(1), place.at_x(3), place.across_y()
    sibling, other_lo = place.sibling(), place.other_y_lo()
    greet(
        [place.at_fellow(k) for k in (1, 2, 3)]
        + [place.at_z(k) for k in range(1, zs)]
        + [right, left, across]
    )
    sender = Sender(send_sems, recv_sems)
    send = sender.send

    plan = reduce_plan(zs)
    last = {}
    slot = 0
    query_copies = []
    for step in range(zs // 2):
        for piece in range(REDUCE_CUTS):
            for chain, (direction, column, hops) in enumerate(plan):
                if step >= hops:
                    continue
                columns = slice(column * HEAD_SIZE, (column + 1) * HEAD_SIZE)
                destination = place.z_at(direction * (hops - step))
                mine = dkv_ref[at(destination * rows + piece * cut, cut), columns]
                if step > 0:
                    copy, before = last[chain, piece]
                    copy.wait_recv()
                    mine = (mine.astype(jnp.float32) + held[before].astype(jnp.float32)).astype(jnp.bfloat16)
                out[slot] = mine
                last[chain, piece] = (send(out.at[slot], held.at[slot], place.at_z(direction)), slot)
                slot += 1
        if step == 0:
            for k in (2, 3, 1):
                query_copies.append(
                    send(
                        dqg_ref.at[at(place.fellow(k) * tokens, tokens)],
                        dq_ref.at[:, at(member * width, width)],
                        place.at_fellow(k),
                    )
                )
    owns, key_copies, value_copies = [], [], []
    for column, target, copies in ((0, key_grad, key_copies), (1, vg_ref, value_copies)):
        columns = slice(column * HEAD_SIZE, (column + 1) * HEAD_SIZE)
        for piece in range(REDUCE_CUTS):
            total = dkv_ref[at(place.z * rows + piece * cut, cut), columns].astype(jnp.float32)
            for chain, (direction, its_column, hops) in enumerate(plan):
                if its_column == column and hops:
                    copy, before = last[chain, piece]
                    copy.wait_recv()
                    total = total + held[before].astype(jnp.float32)
            done[column, piece * cut : (piece + 1) * cut, :] = total.astype(jnp.bfloat16)
        landing = target.at[:, at(member * HEAD_SIZE, HEAD_SIZE)]
        own = pltpu.make_async_copy(
            done.at[column, at(member * tokens, tokens)], landing, own_sems.at[3 + column]
        )
        own.start()
        owns.append(own)
        for k in (2, 3, 1):
            copies.append(
                send(done.at[column, at(place.fellow(k) * tokens, tokens)], landing, place.at_fellow(k))
            )
    loads[0].wait()
    owns[0].wait()
    for copy in key_copies:
        copy.wait_recv()

    kg = key_grad[...]
    lifted = lax.dot_general(
        kg, up_ref[...], (((1,), (1,)), ((), ())), preferred_element_type=jnp.float32
    ).astype(jnp.bfloat16)
    scaled = (lifted.astype(jnp.float32) * ADAPTER_SCALE).astype(jnp.bfloat16)
    rank = lifted.shape[1]
    ranks = rank // 2
    kv_width = kg.shape[1]
    stacked[:, :kv_width] = kg
    stacked[:, kv_width:] = jnp.concatenate([scaled, jnp.zeros_like(scaled)], axis=1)
    up_part = (
        ADAPTER_SCALE
        * lax.dot_general(low_ref[...], kg, (((0,), (0,)), ((), ())), preferred_element_type=jnp.float32)
    ).astype(jnp.bfloat16)
    lanes = parts.shape[3] - 128
    share = kv_width // 8
    padding = jnp.zeros((rank, 128 - share), jnp.bfloat16)
    for f in range(8):
        block = jnp.concatenate([up_part[:, f * share : (f + 1) * share], padding], axis=1)
        parts[f, 0, :, lanes:] = block[:ranks]
        parts[f, 1, :, lanes:] = block[ranks:]

    @pl.loop(0, 8)
    def _(f):
        block = lax.dot_general(
            scaled, inputs[:, at(f * lanes, lanes)], (((0,), (0,)), ((), ())), preferred_element_type=jnp.float32
        ).astype(jnp.bfloat16)
        parts[f, 0, :, :lanes] = block[:ranks]
        parts[f, 1, :, :lanes] = block[ranks:]

    pair_copy = send(parts.at[:, 1 - place.core], pair_in, sibling)
    loads[1].wait()

    def input_gradient(begin, end):
        @pl.loop(begin, end)
        def _(j):
            some = at(j * lanes, lanes)
            grad_ref[:, some] = lax.dot_general(
                stacked[...], full[some, :], (((1,), (1,)), ((), ())), preferred_element_type=jnp.float32
            ).astype(jnp.bfloat16)

    input_gradient(0, 2)
    pair_copy.wait_recv()

    def add(*terms):
        total = terms[0].astype(jnp.float32)
        for term in terms[1:]:
            total = total + term.astype(jnp.float32)
        return total

    @pl.loop(0, 8)
    def _(f):
        row[f] = add(parts[f, pl.ds(place.core, 1)][0], pair_in[f]).astype(jnp.bfloat16)

    here = lambda y_hi, step: place.row(y_hi, place.x + step)
    far_copies = [
        send(row.at[here(0, 2)], far_in.at[0], right),
        send(row.at[here(1, 2)], far_in.at[1], left),
    ]
    near_copies = [
        send(row.at[here(1, 1)], near_in.at[0, 1], right),
        send(row.at[here(0, 3)], near_in.at[1, 0], left),
    ]
    input_gradient(2, 3)
    for way, (y_hi, step, device) in enumerate(((0, 1, right), (1, 3, left))):
        far_copies[way].wait_recv()
        near_out[way] = add(row[here(y_hi, step)], far_in[way]).astype(jnp.bfloat16)
        near_copies.append(send(near_out.at[way], near_in.at[way, y_hi], device))
    input_gradient(3, 5)
    for copy in near_copies:
        copy.wait_recv()

    def over_x(y_hi):
        return add(row[here(y_hi, 0)], near_in[0, y_hi], near_in[1, y_hi])

    y_out[...] = over_x(1 - place.y_hi).astype(jnp.bfloat16)
    y_copy = send(y_out, y_in, across)
    mine = over_x(place.y_hi)
    input_gradient(5, 6)
    y_copy.wait_recv()
    mine = add(mine, y_in[...])
    chunk_lanes = lanes // zs
    cuts = min(zs, 4)
    small = ranks // cuts
    for j in range(zs):
        z_out[j, :ranks] = mine[:, j * chunk_lanes : (j + 1) * chunk_lanes]
        z_out[j, ranks:] = mine[(j % cuts) * small : (j % cuts + 1) * small, lanes:]
    z_copies = []
    for k in sorted(range(1, zs), key=lambda k: -min(k, zs - k)):
        z_copies.append(send(z_out.at[place.z_at(k)], z_in.at[k - 1], place.at_z(k)))
    input_gradient(6, 7)
    for copy in z_copies:
        copy.wait_recv()
    chunk = z_out[place.z]
    for k in range(zs - 1):
        chunk = chunk + z_in[k]
    lo_out[...] = chunk
    lo_copy = send(lo_out, lo_in, other_lo)
    lo_copy.wait_recv()
    chunk = chunk + lo_in[...]
    total_ref[pl.ds(place.core, 1), pl.ds(place.z, 1)] = chunk[None, None]
    block = total_ref.at[place.core, place.z]
    z_copies = []
    for k in sorted(range(1, zs), key=lambda k: -min(k, zs - k)):
        z_copies.append(send(block, block, place.at_z(k)))
    input_gradient(7, 8)
    for copy in z_copies:
        copy.wait_recv()
    block = total_ref.at[place.core]
    send(block, block, sibling).wait_recv()
    for core in range(2):
        for j in range(zs):
            down_ref[core * ranks : (core + 1) * ranks, j * chunk_lanes : (j + 1) * chunk_lanes] = total_ref[
                core, j, :ranks
            ]
        for j in range(cuts):
            begin = core * ranks + j * small
            up_out[begin : begin + small, :] = total_ref[core, j, ranks:, :share]
    for copy in value_copies + query_copies:
        copy.wait_recv()
    sender.finish()
    owns[1].wait()
    own_query.wait()


def dma(count):
    return pltpu.SemaphoreType.DMA((count,))


def params(mebibytes, collective_id=None):
    if collective_id is None:
        return pltpu.CompilerParams(vmem_limit_bytes=mebibytes << 20)
    return pltpu.CompilerParams(
        vmem_limit_bytes=mebibytes << 20, collective_id=collective_id, has_side_effects=True
    )


def body(
    zs,
    inputs,
    queries,
    values,
    output_gradient,
    key_base_weight,
    adapter_down,
    adapter_up,
    span_slot_index,
    segment_document,
):
    bf16, f32, i32 = jnp.bfloat16, jnp.float32, jnp.int32
    rows_in = inputs[0]
    tokens, model = rows_in.shape
    shard, kv_width = key_base_weight.shape
    rank = adapter_down.shape[1]
    length = segment_document.shape[1]
    width = GROUPS * HEAD_SIZE
    half = zs // 2
    shape = jax.ShapeDtypeStruct
    packed_width = kv_width + rank + adapter_up.shape[1]

    copies = 9 + 3 + 6 + 6 + 3 + 4 + 3 + 7 * 4 + 3 + 3 * 2 * half
    full, query_group, gradient_group, value_all, key_all, low_rank, complete_up = pl.pallas_call(
        functools.partial(keys_kernel, zs),
        out_shape=(
            shape((model, packed_width), bf16),
            shape((4 * tokens, width), bf16),
            shape((4 * tokens, width), bf16),
            shape((length, HEAD_SIZE), bf16),
            shape((length, HEAD_SIZE), bf16),
            shape((tokens, rank), bf16),
            shape((rank, kv_width), bf16),
        ),
        in_specs=[ANY, VMEM, VMEM, ANY, ANY, ANY, ANY],
        out_specs=(ANY,) + (VMEM,) * 6,
        scratch_shapes=[
            pltpu.VMEM((model, packed_width), bf16),
            pltpu.VMEM((2 * tokens, model // 2), bf16),
            pltpu.VMEM((2 * tokens, packed_width), f32),
            pltpu.VMEM((tokens, packed_width), f32),
            pltpu.VMEM((tokens, kv_width), bf16),
            dma(copies),
            dma(copies),
            dma(6),
        ],
        compiler_params=params(48, 0),
        name="gather_weights_and_keys",
    )(
        key_base_weight,
        adapter_down.T,
        adapter_up,
        rows_in,
        queries[0],
        output_gradient[0],
        values[0],
    )

    span_rows = 4 * tokens
    tile_rows = (1024 // KEY_TILE + 1, KEY_TILE, GROUPS * SPAN)
    query_grad_group, partial_sums = pl.pallas_call(
        functools.partial(attention_kernel, zs),
        out_shape=(
            jax.ShapeDtypeStruct((span_rows, width), bf16),
            jax.ShapeDtypeStruct((length, 2 * HEAD_SIZE), bf16),
        ),
        in_specs=[SMEM, SMEM] + [VMEM] * 5,
        out_specs=(ANY, VMEM),
        scratch_shapes=[
            pltpu.VMEM((length + KEY_TILE, HEAD_SIZE), bf16),
            pltpu.VMEM((length + KEY_TILE, HEAD_SIZE), bf16),
            pltpu.VMEM((length + KEY_TILE, 2 * HEAD_SIZE), f32),
            pltpu.VMEM(tile_rows, f32),
            pltpu.VMEM(tile_rows, f32),
            pltpu.VMEM((span_rows, width), bf16),
            pltpu.SMEM((span_rows // SPAN,), i32),
            pltpu.VMEM((span_rows // SPAN, 2 * SPAN), i32),
            pltpu.SemaphoreType.DMA,
        ],
        compiler_params=params(24),
        name="attention_gradients",
    )(
        span_slot_index[0],
        segment_document,
        segment_document,
        query_group,
        gradient_group,
        key_all,
        value_all,
    )

    hops = REDUCE_CUTS * sum(hops for _, _, hops in reduce_plan(zs))
    cut = 4 * tokens // REDUCE_CUTS
    ranks = rank // 2
    lanes = shard + 128
    chunk = (ranks + ranks // min(zs, 4), shard // zs)
    copies = hops + 9 + 1 + 6 + 1 + 2 * (zs - 1) + 2
    query_grad, value_grad, input_gradient, down_share, up_share = pl.pallas_call(
        functools.partial(finish_kernel, zs),
        out_shape=(
            shape((tokens, QUERY_HEADS * HEAD_SIZE), bf16),
            shape((tokens, kv_width), bf16),
            shape((tokens, model), bf16),
            shape((rank, shard), f32),
            shape((rank, adapter_up.shape[1]), f32),
        ),
        in_specs=[VMEM, ANY, VMEM, VMEM, HBM, HBM],
        out_specs=(ANY, ANY, VMEM, VMEM, VMEM),
        scratch_shapes=[
            pltpu.VMEM((2, zs) + chunk, f32),
            pltpu.VMEM((hops, cut, HEAD_SIZE), bf16),
            pltpu.VMEM((hops, cut, HEAD_SIZE), bf16),
            pltpu.VMEM((2, 4 * tokens, HEAD_SIZE), bf16),
            pltpu.VMEM((tokens, kv_width), bf16),
            pltpu.VMEM((tokens, model), bf16),
            pltpu.VMEM((model, packed_width), bf16),
            pltpu.VMEM((tokens, packed_width), bf16),
            pltpu.VMEM((8, 2, ranks, lanes), bf16),
            pltpu.VMEM((8, ranks, lanes), bf16),
            pltpu.VMEM((8, ranks, lanes), bf16),
            pltpu.VMEM((2, ranks, lanes), bf16),
            pltpu.VMEM((2, ranks, lanes), bf16),
            pltpu.VMEM((2, 2, ranks, lanes), bf16),
            pltpu.VMEM((ranks, lanes), bf16),
            pltpu.VMEM((ranks, lanes), bf16),
            pltpu.VMEM((zs,) + chunk, f32),
            pltpu.VMEM((zs - 1,) + chunk, f32),
            pltpu.VMEM(chunk, f32),
            pltpu.VMEM(chunk, f32),
            dma(copies),
            dma(copies),
            dma(5),
        ],
        compiler_params=params(44, 1),
        name="sum_gradients",
    )(partial_sums, query_grad_group, low_rank, complete_up, rows_in, full)

    return (query_grad[None], value_grad[None], input_gradient[None], down_share.T, up_share)


def solution(mesh):
    spread, rows = P("fsdp", "context", None), P("fsdp", None)
    placed = (spread, spread, spread, spread, rows, rows, P(None, "fsdp"), rows, rows)
    return jax.shard_map(
        functools.partial(body, mesh.shape["context"] // 4),
        mesh=mesh,
        in_specs=placed,
        out_specs=(spread, spread, spread, rows, P(None, "fsdp")),
        check_vma=False,
    )
```

```python
import functools
import math

import jax
import jax.numpy as jnp
from jax import lax
from jax.experimental import pallas as pl
from jax.experimental.pallas import tpu as pltpu
from jax.sharding import PartitionSpec as P

QUERY_HEADS = 32
KEY_VALUE_HEADS = 4
HEAD_SIZE = 128
GROUPS = QUERY_HEADS // KEY_VALUE_HEADS
SPAN = 64
ADAPTER_SCALE = 0.5
NEGATIVE_FILL = -1e30
KEY_TILE = 256
MESH = pl.DeviceIdType.MESH
ANY = pl.BlockSpec(memory_space=pl.ANY)
VMEM = pl.BlockSpec(memory_space=pltpu.VMEM)
HBM = pl.BlockSpec(memory_space=pltpu.HBM)
SMEM = pl.BlockSpec(memory_space=pltpu.SMEM)


def at(start, size):
    return pl.ds(pl.multiple_of(start, size), size)


class Place:
    def __init__(self, zs):
        self.zs = zs
        self.fsdp = lax.axis_index("fsdp")
        self.context = lax.axis_index("context")
        self.y_hi, self.x = lax.div(self.fsdp, 4), lax.rem(self.fsdp, 4)
        self.z, self.member = lax.div(self.context, 4), lax.rem(self.context, 4)
        self.y_lo, self.core = lax.div(self.member, 2), lax.rem(self.member, 2)

    def row(self, y_hi, x):
        return y_hi * 4 + lax.rem(x, 4)

    def at_x(self, step):
        return {"fsdp": self.row(self.y_hi, self.x + step), "context": self.context}

    def across_y(self):
        return {
            "fsdp": self.row(1 - self.y_hi, self.x),
            "context": self.z * 4 + (1 - self.y_lo) * 2 + self.core,
        }

    def other_y_lo(self):
        return self.of_context(self.z * 4 + (1 - self.y_lo) * 2 + self.core)

    def sibling(self):
        return self.of_context(self.z * 4 + self.y_lo * 2 + 1 - self.core)

    def of_context(self, context):
        return {"fsdp": self.fsdp, "context": context}

    def fellow(self, k):
        return lax.rem(self.member + k, 4)

    def at_fellow(self, k):
        return self.of_context(self.z * 4 + self.fellow(k))

    def z_at(self, step):
        return lax.rem(self.z + step + self.zs, self.zs)

    def at_z(self, step):
        return self.of_context(self.z_at(step) * 4 + self.member)


def greet(partners):
    barrier = pltpu.get_barrier_semaphore()
    for partner in partners:
        pl.semaphore_signal(barrier, inc=1, device_id=partner, device_id_type=MESH)
    pl.semaphore_wait(barrier, len(partners))


class Sender:
    def __init__(self, send_sems, recv_sems):
        self.send_sems, self.recv_sems, self.copies = send_sems, recv_sems, []

    def send(self, src, dst, device):
        k = len(self.copies)
        assert k < self.send_sems.shape[0]
        copy = pltpu.make_async_remote_copy(
            src_ref=src,
            dst_ref=dst,
            send_sem=self.send_sems.at[k],
            recv_sem=self.recv_sems.at[k],
            device_id=device,
            device_id_type=MESH,
        )
        copy.start()
        self.copies.append(copy)
        return copy

    def finish(self):
        for copy in self.copies:
            copy.wait_send()


class Ring:
    def __init__(self, place, sender, buffer, block, rows):
        self.place, self.sender, self.buffer = place, sender, buffer
        self.block, self.rows, self.stage, self.flying = block, rows, 0, ()
        self.stages = place.zs // 2

    def step(self):
        for copy in self.flying:
            copy.wait_recv()
        self.flying = ()
        if self.stage == self.stages:
            return
        right_at, left_at = self.block(self.place.z_at(-self.stage)), self.block(self.place.z_at(self.stage))
        if self.stage < self.stages - 1:
            right_rows, left_rows = at(right_at, self.rows), at(left_at, self.rows)
        else:
            cut = self.rows // 2
            right_rows, left_rows = at(right_at, cut), at(left_at + cut, cut)
        buffer, send = self.buffer, self.sender.send
        self.flying = (
            send(buffer.at[right_rows], buffer.at[right_rows], self.place.at_z(1)),
            send(buffer.at[left_rows], buffer.at[left_rows], self.place.at_z(-1)),
        )
        self.stage += 1

    def run(self):
        while self.stage < self.stages or self.flying:
            self.step()


def keys_kernel(
    zs,
    w_hbm,
    d_ref,
    u_ref,
    x_hbm,
    q_ref,
    g_ref,
    v_ref,
    full_ref,
    qg_ref,
    gg_ref,
    vg_ref,
    kg_ref,
    low_ref,
    up_ref,
    full,
    inputs,
    projected,
    pair_in,
    keys,
    send_sems,
    recv_sems,
    own_sems,
):
    place = Place(zs)
    tokens = q_ref.shape[0]
    shard, kv_width = w_hbm.shape
    rank = d_ref.shape[0]
    unit = shard // 8
    width = GROUPS * HEAD_SIZE
    member = place.member
    mine = at((place.z * 4 + member) * tokens, tokens)
    columns = at(member * HEAD_SIZE, HEAD_SIZE)
    piece = shard // 2

    def columns_of(f, core):
        return at(f * shard + core * piece, piece)

    def own_inputs(f):
        return pltpu.make_async_copy(
            x_hbm.at[:, columns_of(f, place.core)],
            inputs.at[:tokens, f * piece : (f + 1) * piece],
            own_sems.at[0],
        )

    for f in range(8):
        own_inputs(f).start()
    owns = [
        pltpu.make_async_copy(
            q_ref.at[:, at(member * width, width)], qg_ref.at[at(member * tokens, tokens)], own_sems.at[1]
        ),
        pltpu.make_async_copy(
            g_ref.at[:, at(member * width, width)], gg_ref.at[at(member * tokens, tokens)], own_sems.at[2]
        ),
        pltpu.make_async_copy(v_ref.at[:, columns], vg_ref.at[mine], own_sems.at[3]),
    ]
    for own in owns:
        own.start()
    own_rows = at(place.fsdp * shard, shard)
    weights = pltpu.make_async_copy(w_hbm, full.at[own_rows, :kv_width], own_sems.at[5])
    weights.start()
    filler = jnp.zeros((shard // 2 - rank, u_ref.shape[1]), jnp.bfloat16)
    up_rows = jnp.concatenate([u_ref[...], filler] * 2, axis=0)
    full[own_rows, kv_width:] = jnp.concatenate([d_ref[...].T, up_rows], axis=1)
    projected[...] = jnp.zeros_like(projected)
    weights.wait()

    right, left, across, sibling = place.at_x(1), place.at_x(3), place.across_y(), place.sibling()
    z_up, z_down = place.at_z(1), place.at_z(-1)
    greet([right, left, across] + [place.at_fellow(k) for k in (1, 2, 3)] + [z_up, z_down])
    sender = Sender(send_sems, recv_sems)
    send = sender.send

    parity = lax.rem(place.z, 2)

    def rows_of(f, offset, size):
        begin = f * shard + place.core * 4 * unit + offset
        return full.at[pl.ds(pl.multiple_of(begin, unit // 2), size)]

    def bridge(f):
        return rows_of(f, parity * 3 * unit, unit)

    def body(f):
        return rows_of(f, unit, 2 * unit)

    def low_body(f):
        return rows_of(f, unit, unit // 2)

    def high_body(f):
        return rows_of(f, unit + unit // 2, 3 * unit // 2)

    def pass_on(block, *devices):
        return [send(block, block, device) for device in devices]

    y_hi, x = place.y_hi, place.x
    row = lambda y, step: place.row(y, x + step)
    own, near_left, near_right, far = (row(y_hi, k) for k in (0, 3, 1, 2))
    over, over_left, over_right, over_far = (row(1 - y_hi, k) for k in (0, 3, 1, 2))

    sibling_inputs = [
        send(
            x_hbm.at[:, columns_of(f, 1 - place.core)],
            inputs.at[tokens:, f * piece : (f + 1) * piece],
            sibling,
        )
        for f in range(8)
    ]
    value_copies = [
        send(
            v_ref.at[:, at(place.fellow(k) * HEAD_SIZE, HEAD_SIZE)], vg_ref.at[mine], place.at_fellow(k)
        )
        for k in (1, 2, 3)
    ]
    near_left_bridge, near_right_bridge, over_bridge = pass_on(bridge(own), right, left, across)
    near_left_body, near_right_body, over_body = pass_on(body(own), right, left, across)
    shares = {}
    crossing = {}

    def share(name, f):
        shares[name] = pass_on(rows_of(f, parity * unit, 3 * unit), sibling)[0]

    def cross(name, f):
        begin = parity * 3 * unit
        crossing[name] = (
            pass_on(rows_of(f, begin, unit // 2), z_up)
            + pass_on(rows_of(f, begin + unit // 2, unit // 2), z_down)
        )

    def land(name, f):
        for copy in crossing[name]:
            copy.wait_recv()
        shares[name, "rest"] = pass_on(rows_of(f, (1 - parity) * 3 * unit, unit), sibling)[0]

    def multiply(f, offset, size):
        columns = pl.ds(pl.multiple_of(f * piece + offset, unit), size)
        projected[...] += jnp.dot(
            inputs[:, columns], rows_of(f, offset, size)[...], preferred_element_type=jnp.float32
        )

    def project(f):
        multiply(f, parity * unit, 3 * unit)

    def project_rest(f):
        multiply(f, (1 - parity) * 3 * unit, unit)

    pltpu.make_async_copy(x_hbm.at[:, : 8 * piece], inputs.at[:tokens], own_sems.at[0]).wait()
    for copy in sibling_inputs:
        copy.wait_recv()
    multiply(own, 0, 4 * unit)

    near_left_bridge.wait_recv()
    far_bridge = pass_on(bridge(near_left), right)[0]
    cross("near_left", near_left)
    near_right_bridge.wait_recv()
    cross("near_right", near_right)
    over_bridge.wait_recv()
    over_left_bridge, over_right_bridge = pass_on(bridge(over), right, left)
    cross("over", over)
    head_copies = []
    for k in (2, 3, 1):
        for src, dst in ((q_ref, qg_ref), (g_ref, gg_ref)):
            head_copies.append(
                send(
                    src.at[:, at(place.fellow(k) * width, width)],
                    dst.at[at(member * tokens, tokens)],
                    place.at_fellow(k),
                )
            )

    near_left_body.wait_recv()
    far_low = pass_on(low_body(near_left), right)[0]
    near_right_body.wait_recv()
    far_high = pass_on(high_body(near_right), left)[0]
    over_body.wait_recv()
    over_left_body, over_right_body = pass_on(body(over), right, left)
    share("near_left", near_left)
    share("near_right", near_right)
    share("over", over)
    far_bridge.wait_recv()
    over_far_bridge = pass_on(bridge(far), across)[0]
    cross("far", far)
    far_low.wait_recv()
    over_far_low = pass_on(low_body(far), across)[0]
    for name, f in (("near_left", near_left), ("near_right", near_right), ("over", over)):
        land(name, f)
    far_high.wait_recv()
    over_far_high = pass_on(high_body(far), across)[0]
    share("far", far)
    for copy in value_copies:
        copy.wait_recv()
    owns[2].wait()
    ring = Ring(place, sender, vg_ref, lambda z: z * 4 * tokens, 4 * tokens)
    ring.step()
    over_left_bridge.wait_recv()
    cross("over_left", over_left)
    over_right_bridge.wait_recv()
    cross("over_right", over_right)
    over_far_bridge.wait_recv()
    cross("over_far", over_far)
    land("far", far)
    for f in (near_left, near_right, over, far):
        project(f)
        project_rest(f)
    over_left_body.wait_recv()
    project(over_left)
    share("over_left", over_left)
    over_right_body.wait_recv()
    project(over_right)
    share("over_right", over_right)
    ring.step()
    for name, f in (("over_left", over_left), ("over_right", over_right), ("over_far", over_far)):
        land(name, f)
        project_rest(f)
    over_far_low.wait_recv()
    over_far_high.wait_recv()
    project(over_far)
    pair_copy = send(projected.at[tokens:], pair_in, sibling)
    share("over_far", over_far)

    def stores(core):
        for f in range(8):
            rows = columns_of(f, core)
            pltpu.make_async_copy(full.at[rows], full_ref.at[rows], own_sems.at[0]).start()

    stores(place.core)
    ring.step()
    pair_copy.wait_recv()
    projection = projected[:tokens] + pair_in[...]

    low_rank = projection[:, kv_width : kv_width + rank].astype(jnp.bfloat16)
    low_ref[...] = low_rank
    for f in range(8):
        up_ref[:, f * (kv_width // 8) : (f + 1) * (kv_width // 8)] = full[
            at(f * shard + place.core * piece, rank), kv_width + rank :
        ]
    keys[...] = (
        projection[:, :kv_width]
        + ADAPTER_SCALE * jnp.dot(low_rank, up_ref[...], preferred_element_type=jnp.float32)
    ).astype(jnp.bfloat16)
    own_keys = pltpu.make_async_copy(keys.at[:, columns], kg_ref.at[mine], own_sems.at[4])
    own_keys.start()

    def exchange(device, fellow):
        return send(keys.at[:, at(fellow * HEAD_SIZE, HEAD_SIZE)], kg_ref.at[mine], device)

    to_sibling = exchange(sibling, member + 1 - 2 * place.core)
    other = [
        exchange(place.at_fellow(k), place.fellow(k)) for k in (2,)
    ]
    third = lax.rem(member + 3 - 2 * place.core, 4)
    other.append(exchange(place.of_context(place.z * 4 + third), third))
    rings = [
        Ring(place, sender, kg_ref, lambda z: (z * 4 + place.y_lo * 2) * tokens, 2 * tokens),
        Ring(place, sender, kg_ref, lambda z: (z * 4 + (1 - place.y_lo) * 2) * tokens, 2 * tokens),
    ]
    to_sibling.wait_recv()
    own_keys.wait()
    rings[0].step()
    for copy in other:
        copy.wait_recv()
    rings[1].step()
    for copy in shares.values():
        copy.wait_recv()
    stores(1 - place.core)
    rings.append(ring)
    ring.step()
    while any(some.flying for some in rings):
        for some in rings:
            some.step()
    for copy in head_copies:
        copy.wait_recv()
    sender.finish()
    owns[0].wait()
    owns[1].wait()
    pltpu.make_async_copy(full, full_ref, own_sems.at[0]).wait()


def attention_kernel(
    zs,
    list_ref,
    doc_smem,
    doc_ref,
    queries,
    gradients,
    k_ref,
    v_ref,
    dq_hbm,
    dkv_ref,
    keys,
    values,
    totals,
    scores,
    grads,
    dq_rows,
    q_columns,
    g_columns,
    firsts,
    starts,
    store_sem,
):
    to_exponent = math.log2(math.e) / math.sqrt(HEAD_SIZE)
    inv_root = 1.0 / math.sqrt(HEAD_SIZE)
    lanes = GROUPS * SPAN
    spans = list_ref.shape[0]
    own_spans = queries.shape[0] // SPAN
    z = lax.div(lax.axis_index("context"), 4)
    length = spans * SPAN

    keys[length:, :] = jnp.zeros((KEY_TILE, HEAD_SIZE), jnp.bfloat16)
    values[length:, :] = jnp.zeros((KEY_TILE, HEAD_SIZE), jnp.bfloat16)

    @pl.loop(0, spans + KEY_TILE // SPAN)
    def _(n):
        totals[at(n * SPAN, SPAN), :] = jnp.zeros((SPAN, 2 * HEAD_SIZE), jnp.float32)

    def document_start(position):
        document = doc_smem[0, position]

        def narrow(_, carry):
            low, high = carry
            middle = lax.shift_right_logical(low + high, 1)
            earlier = doc_smem[0, middle] < document
            return jnp.where(earlier, middle + 1, low), jnp.where(earlier, high, middle)

        return lax.fori_loop(0, 12, narrow, (jnp.maximum(position - 1024, 0), position))[0]

    shape = (own_spans, 2 * SPAN)
    row = lax.broadcasted_iota(jnp.int32, shape, 0)
    lane = lax.broadcasted_iota(jnp.int32, shape, 1)
    row_begin, row_first = jnp.zeros(shape, jnp.int32), jnp.zeros(shape, jnp.int32)
    for i in range(own_spans):
        slot = list_ref[z * own_spans + i]
        begin = lax.shift_right_logical(slot, 1) * 2 * SPAN
        starts[i : i + 1, :] = doc_ref[0:1, pl.ds(pl.multiple_of(begin, 2 * SPAN), 2 * SPAN)]
        row_begin = jnp.where(row == i, begin, row_begin)
        row_first = jnp.where(row == i, document_start(begin), row_first)
        firsts[i] = lax.shift_right_logical(document_start(slot * SPAN), 6)
    documents = starts[...]
    changes = jnp.where((lane > 0) & (documents != pltpu.roll(documents, 1, 1)), lane, 0)
    for step in (1, 2, 4, 8, 16, 32, 64):
        changes = jnp.maximum(changes, jnp.where(lane >= step, pltpu.roll(changes, step, 1), 0))
    starts[...] = jnp.where(changes == 0, row_first, row_begin + changes)

    @pl.loop(0, spans)
    def _(s):
        src, dst = at(s * SPAN, SPAN), at(list_ref[s] * SPAN, SPAN)
        keys[dst, :] = k_ref[src, :]
        values[dst, :] = v_ref[src, :]

    @pl.loop(0, own_spans)
    def _(i):
        slot, first = list_ref[z * own_spans + i], firsts[i]
        own = at(i * SPAN, SPAN)
        q_rows = jnp.concatenate(
            [queries[own, g * HEAD_SIZE : (g + 1) * HEAD_SIZE] for g in range(GROUPS)], axis=0
        )
        g_rows = jnp.concatenate(
            [gradients[own, g * HEAD_SIZE : (g + 1) * HEAD_SIZE] for g in range(GROUPS)], axis=0
        )
        pair = starts[pl.ds(i, 1), :]
        own_start = jnp.where(lax.rem(slot, 2) == 1, pair[:, SPAN:], pair[:, :SPAN])
        q_columns[...] = q_rows.T
        g_columns[...] = g_rows.T
        q_start = jnp.concatenate([own_start] * GROUPS, axis=1) - first * SPAN
        lane = lax.broadcasted_iota(jnp.int32, (1, lanes), 1)
        q_pos = (slot - first) * SPAN + lax.rem(lane, SPAN)
        tiles = lax.div(slot - first + KEY_TILE // SPAN, KEY_TILE // SPAN)

        def rows_at(t, first=first):
            return pl.ds(pl.multiple_of(first * SPAN + t * KEY_TILE, SPAN), KEY_TILE)

        def peak_step(t, peak, q_rows=q_rows, q_start=q_start, q_pos=q_pos, rows_at=rows_at):
            raw = jnp.dot(keys[rows_at(t), :], q_columns[...], preferred_element_type=jnp.float32)
            key_pos = lax.broadcasted_iota(jnp.int32, (KEY_TILE, lanes), 0)
            raw = jnp.where(
                (key_pos >= q_start - t * KEY_TILE) & (key_pos <= q_pos - t * KEY_TILE), raw, NEGATIVE_FILL
            )
            scores[t] = raw
            grads[t] = jnp.dot(values[rows_at(t), :], g_columns[...], preferred_element_type=jnp.float32)
            return jnp.maximum(peak, jnp.max(raw, axis=0, keepdims=True))

        peak = lax.fori_loop(0, tiles, peak_step, jnp.full((1, lanes), NEGATIVE_FILL, jnp.float32))

        def sum_step(t, carry, peak=peak):
            normalizer, weighted = carry
            weights = jnp.exp2((scores[t] - peak) * to_exponent)
            scores[t] = weights
            return (
                normalizer + jnp.sum(weights, axis=0, keepdims=True),
                weighted + jnp.sum(weights * grads[t], axis=0, keepdims=True),
            )

        zero = jnp.zeros((1, lanes), jnp.float32)
        normalizer, weighted = lax.fori_loop(0, tiles, sum_step, (zero, zero))
        inverse = 1.0 / normalizer
        row_terms = weighted * inverse

        def grad_step(t, dq, q_rows=q_rows, g_rows=g_rows, inverse=inverse, row_terms=row_terms, rows_at=rows_at):
            rows = rows_at(t)
            probability = scores[t] * inverse
            dscore = (probability * (grads[t] - row_terms) * inv_root).astype(jnp.bfloat16)
            prob_low = probability.astype(jnp.bfloat16)
            totals[rows, :HEAD_SIZE] += jnp.dot(dscore, q_rows, preferred_element_type=jnp.float32)
            totals[rows, HEAD_SIZE:] += jnp.dot(prob_low, g_rows, preferred_element_type=jnp.float32)
            return dq + lax.dot_general(
                keys[rows, :], dscore, (((0,), (0,)), ((), ())), preferred_element_type=jnp.float32
            )

        dq = lax.fori_loop(0, tiles, grad_step, jnp.zeros((HEAD_SIZE, lanes), jnp.float32))
        dq = dq.T.astype(jnp.bfloat16)
        for g in range(GROUPS):
            dq_rows[own, g * HEAD_SIZE : (g + 1) * HEAD_SIZE] = dq[g * SPAN : (g + 1) * SPAN]
        pltpu.make_async_copy(dq_rows.at[own], dq_hbm.at[own], store_sem).start()

    @pl.loop(0, spans)
    def _(s):
        dkv_ref[at(s * SPAN, SPAN), :] = totals[at(list_ref[s] * SPAN, SPAN), :].astype(jnp.bfloat16)

    pltpu.make_async_copy(dq_rows, dq_hbm, store_sem).wait()


REDUCE_CUTS = 2


def reduce_plan(zs):
    half = zs // 2
    return [(1, 0, half), (-1, 1, half), (-1, 0, half - 1), (1, 1, half - 1)]


def finish_kernel(
    zs,
    dkv_ref,
    dqg_ref,
    low_ref,
    up_ref,
    x_hbm,
    full_hbm,
    dq_ref,
    vg_ref,
    grad_ref,
    down_ref,
    up_out,
    total_ref,
    out,
    held,
    done,
    key_grad,
    inputs,
    full,
    stacked,
    parts,
    pair_in,
    row,
    far_in,
    near_out,
    near_in,
    y_out,
    y_in,
    z_out,
    z_in,
    send_sems,
    recv_sems,
    own_sems,
):
    place = Place(zs)
    tokens = dq_ref.shape[0]
    width = GROUPS * HEAD_SIZE
    member = place.member
    rows = 4 * tokens
    cut = rows // REDUCE_CUTS
    loads = [
        pltpu.make_async_copy(x_hbm, inputs, own_sems.at[0]),
        pltpu.make_async_copy(full_hbm, full, own_sems.at[1]),
    ]
    for load in loads:
        load.start()
    own_query = pltpu.make_async_copy(
        dqg_ref.at[at(member * tokens, tokens)], dq_ref.at[:, at(member * width, width)], own_sems.at[2]
    )
    own_query.start()
    right, left, across = place.at_x(1), place.at_x(3), place.across_y()
    sibling, other_lo = place.sibling(), place.other_y_lo()
    beyond = {"fsdp": place.row(1 - place.y_hi, place.x), "context": place.context}
    greet(
        [place.at_fellow(k) for k in (1, 2, 3)]
        + [place.at_z(k) for k in range(1, zs)]
        + [right, left, across, beyond]
    )
    sender = Sender(send_sems, recv_sems)
    send = sender.send

    plan = reduce_plan(zs)
    last = {}
    slot = 0
    query_copies = []
    for step in range(zs // 2):
        for piece in range(REDUCE_CUTS):
            for chain, (direction, column, hops) in enumerate(plan):
                if step >= hops:
                    continue
                columns = slice(column * HEAD_SIZE, (column + 1) * HEAD_SIZE)
                destination = place.z_at(direction * (hops - step))
                mine = dkv_ref[at(destination * rows + piece * cut, cut), columns]
                if step > 0:
                    copy, before = last[chain, piece]
                    copy.wait_recv()
                    mine = (mine.astype(jnp.float32) + held[before].astype(jnp.float32)).astype(jnp.bfloat16)
                out[slot] = mine
                last[chain, piece] = (send(out.at[slot], held.at[slot], place.at_z(direction)), slot)
                slot += 1
        if step == 0:
            for k in (2, 3, 1):
                query_copies.append(
                    send(
                        dqg_ref.at[at(place.fellow(k) * tokens, tokens)],
                        dq_ref.at[:, at(member * width, width)],
                        place.at_fellow(k),
                    )
                )
    owns, key_copies, value_copies = [], [], []
    for column, target, copies in ((0, key_grad, key_copies), (1, vg_ref, value_copies)):
        columns = slice(column * HEAD_SIZE, (column + 1) * HEAD_SIZE)
        for piece in range(REDUCE_CUTS):
            total = dkv_ref[at(place.z * rows + piece * cut, cut), columns].astype(jnp.float32)
            for chain, (direction, its_column, hops) in enumerate(plan):
                if its_column == column and hops:
                    copy, before = last[chain, piece]
                    copy.wait_recv()
                    total = total + held[before].astype(jnp.float32)
            done[column, piece * cut : (piece + 1) * cut, :] = total.astype(jnp.bfloat16)
        landing = target.at[:, at(member * HEAD_SIZE, HEAD_SIZE)]
        own = pltpu.make_async_copy(
            done.at[column, at(member * tokens, tokens)], landing, own_sems.at[3 + column]
        )
        own.start()
        owns.append(own)
        for k in (2, 3, 1):
            copies.append(
                send(done.at[column, at(place.fellow(k) * tokens, tokens)], landing, place.at_fellow(k))
            )
    loads[0].wait()
    owns[0].wait()
    for copy in key_copies:
        copy.wait_recv()

    kg = key_grad[...]
    lifted = lax.dot_general(
        kg, up_ref[...], (((1,), (1,)), ((), ())), preferred_element_type=jnp.float32
    ).astype(jnp.bfloat16)
    scaled = (lifted.astype(jnp.float32) * ADAPTER_SCALE).astype(jnp.bfloat16)
    rank = lifted.shape[1]
    ranks = rank // 2
    kv_width = kg.shape[1]
    stacked[:, :kv_width] = kg
    stacked[:, kv_width:] = jnp.concatenate([scaled, jnp.zeros_like(scaled)], axis=1)
    up_part = (
        ADAPTER_SCALE
        * lax.dot_general(low_ref[...], kg, (((0,), (0,)), ((), ())), preferred_element_type=jnp.float32)
    ).astype(jnp.bfloat16)
    lanes = parts.shape[3] - 128
    share = kv_width // 8
    padding = jnp.zeros((rank, 128 - share), jnp.bfloat16)
    for f in range(8):
        block = jnp.concatenate([up_part[:, f * share : (f + 1) * share], padding], axis=1)
        parts[f, 0, :, lanes:] = block[:ranks]
        parts[f, 1, :, lanes:] = block[ranks:]

    @pl.loop(0, 8)
    def _(f):
        block = lax.dot_general(
            scaled, inputs[:, at(f * lanes, lanes)], (((0,), (0,)), ((), ())), preferred_element_type=jnp.float32
        ).astype(jnp.bfloat16)
        parts[f, 0, :, :lanes] = block[:ranks]
        parts[f, 1, :, :lanes] = block[ranks:]

    pair_copy = send(parts.at[:, 1 - place.core], pair_in, sibling)
    loads[1].wait()

    def input_gradient(begin, end):
        @pl.loop(begin, end)
        def _(j):
            some = at(j * lanes, lanes)
            grad_ref[:, some] = lax.dot_general(
                stacked[...], full[some, :], (((1,), (1,)), ((), ())), preferred_element_type=jnp.float32
            ).astype(jnp.bfloat16)

    input_gradient(0, 2)
    pair_copy.wait_recv()

    def add(*terms):
        total = terms[0].astype(jnp.float32)
        for term in terms[1:]:
            total = total + term.astype(jnp.float32)
        return total

    @pl.loop(0, 8)
    def _(f):
        row[f] = add(parts[f, pl.ds(place.core, 1)][0], pair_in[f]).astype(jnp.bfloat16)

    here = lambda y_hi, step: place.row(y_hi, place.x + step)
    far_copies = [
        send(row.at[here(0, 2)], far_in.at[0], right),
        send(row.at[here(1, 2)], far_in.at[1], left),
    ]
    near_copies = [
        send(row.at[here(1, 1)], near_in.at[0, 1], right),
        send(row.at[here(0, 3)], near_in.at[1, 0], left),
    ]
    input_gradient(2, 3)
    for way, (y_hi, step, device) in enumerate(((0, 1, right), (1, 3, left))):
        far_copies[way].wait_recv()
        near_out[way] = add(row[here(y_hi, step)], far_in[way]).astype(jnp.bfloat16)
        near_copies.append(send(near_out.at[way], near_in.at[way, y_hi], device))
    input_gradient(3, 5)
    for copy in near_copies:
        copy.wait_recv()

    def over_x(y_hi):
        return add(row[here(y_hi, 0)], near_in[0, y_hi], near_in[1, y_hi])

    y_out[0] = over_x(1 - place.y_hi).astype(jnp.bfloat16)
    y_copies = [send(y_out.at[0], y_in.at[0], beyond), send(y_out.at[0], y_in.at[1], across)]
    mine = over_x(place.y_hi)
    y_out[1] = mine.astype(jnp.bfloat16)
    y_copies.append(send(y_out.at[1], y_in.at[2], other_lo))
    input_gradient(5, 6)
    for copy in y_copies:
        copy.wait_recv()
    mine = add(mine, y_in[0], y_in[1], y_in[2])
    chunk_lanes = lanes // zs
    cuts = min(zs, 4)
    small = ranks // cuts
    for j in range(zs):
        z_out[j, :ranks] = mine[:, j * chunk_lanes : (j + 1) * chunk_lanes]
        z_out[j, ranks:] = mine[(j % cuts) * small : (j % cuts + 1) * small, lanes:]
    z_copies = []
    for k in sorted(range(1, zs), key=lambda k: -min(k, zs - k)):
        z_copies.append(send(z_out.at[place.z_at(k)], z_in.at[k - 1], place.at_z(k)))
    input_gradient(6, 7)
    for copy in z_copies:
        copy.wait_recv()
    chunk = z_out[place.z]
    for k in range(zs - 1):
        chunk = chunk + z_in[k]
    total_ref[pl.ds(place.core, 1), pl.ds(place.z, 1)] = chunk[None, None]
    block = total_ref.at[place.core, place.z]
    z_copies = []
    for k in sorted(range(1, zs), key=lambda k: -min(k, zs - k)):
        z_copies.append(send(block, block, place.at_z(k)))
    input_gradient(7, 8)
    for copy in z_copies:
        copy.wait_recv()
    block = total_ref.at[place.core]
    send(block, block, sibling).wait_recv()
    for core in range(2):
        for j in range(zs):
            down_ref[core * ranks : (core + 1) * ranks, j * chunk_lanes : (j + 1) * chunk_lanes] = total_ref[
                core, j, :ranks
            ]
        for j in range(cuts):
            begin = core * ranks + j * small
            up_out[begin : begin + small, :] = total_ref[core, j, ranks:, :share]
    for copy in value_copies + query_copies:
        copy.wait_recv()
    sender.finish()
    owns[1].wait()
    own_query.wait()


def dma(count):
    return pltpu.SemaphoreType.DMA((count,))


def params(mebibytes, collective_id=None):
    if collective_id is None:
        return pltpu.CompilerParams(vmem_limit_bytes=mebibytes << 20)
    return pltpu.CompilerParams(
        vmem_limit_bytes=mebibytes << 20, collective_id=collective_id, has_side_effects=True
    )


def body(
    zs,
    inputs,
    queries,
    values,
    output_gradient,
    key_base_weight,
    adapter_down,
    adapter_up,
    span_slot_index,
    segment_document,
):
    bf16, f32, i32 = jnp.bfloat16, jnp.float32, jnp.int32
    rows_in = inputs[0]
    tokens, model = rows_in.shape
    shard, kv_width = key_base_weight.shape
    rank = adapter_down.shape[1]
    length = segment_document.shape[1]
    width = GROUPS * HEAD_SIZE
    half = zs // 2
    shape = jax.ShapeDtypeStruct
    packed_width = kv_width + rank + adapter_up.shape[1]

    copies = 9 + 3 + 6 + 6 + 3 + 4 + 3 + 7 * 4 + 3 + 3 * 2 * half
    full, query_group, gradient_group, value_all, key_all, low_rank, complete_up = pl.pallas_call(
        functools.partial(keys_kernel, zs),
        out_shape=(
            shape((model, packed_width), bf16),
            shape((4 * tokens, width), bf16),
            shape((4 * tokens, width), bf16),
            shape((length, HEAD_SIZE), bf16),
            shape((length, HEAD_SIZE), bf16),
            shape((tokens, rank), bf16),
            shape((rank, kv_width), bf16),
        ),
        in_specs=[ANY, VMEM, VMEM, ANY, ANY, ANY, ANY],
        out_specs=(ANY,) + (VMEM,) * 6,
        scratch_shapes=[
            pltpu.VMEM((model, packed_width), bf16),
            pltpu.VMEM((2 * tokens, model // 2), bf16),
            pltpu.VMEM((2 * tokens, packed_width), f32),
            pltpu.VMEM((tokens, packed_width), f32),
            pltpu.VMEM((tokens, kv_width), bf16),
            dma(copies),
            dma(copies),
            dma(6),
        ],
        compiler_params=params(48, 0),
        name="gather_weights_and_keys",
    )(
        key_base_weight,
        adapter_down.T,
        adapter_up,
        rows_in,
        queries[0],
        output_gradient[0],
        values[0],
    )

    span_rows = 4 * tokens
    tile_rows = (1024 // KEY_TILE + 1, KEY_TILE, GROUPS * SPAN)
    query_grad_group, partial_sums = pl.pallas_call(
        functools.partial(attention_kernel, zs),
        out_shape=(
            jax.ShapeDtypeStruct((span_rows, width), bf16),
            jax.ShapeDtypeStruct((length, 2 * HEAD_SIZE), bf16),
        ),
        in_specs=[SMEM, SMEM] + [VMEM] * 5,
        out_specs=(ANY, VMEM),
        scratch_shapes=[
            pltpu.VMEM((length + KEY_TILE, HEAD_SIZE), bf16),
            pltpu.VMEM((length + KEY_TILE, HEAD_SIZE), bf16),
            pltpu.VMEM((length + KEY_TILE, 2 * HEAD_SIZE), f32),
            pltpu.VMEM(tile_rows, f32),
            pltpu.VMEM(tile_rows, f32),
            pltpu.VMEM((span_rows, width), bf16),
            pltpu.VMEM((HEAD_SIZE, GROUPS * SPAN), bf16),
            pltpu.VMEM((HEAD_SIZE, GROUPS * SPAN), bf16),
            pltpu.SMEM((span_rows // SPAN,), i32),
            pltpu.VMEM((span_rows // SPAN, 2 * SPAN), i32),
            pltpu.SemaphoreType.DMA,
        ],
        compiler_params=params(24),
        name="attention_gradients",
    )(
        span_slot_index[0],
        segment_document,
        segment_document,
        query_group,
        gradient_group,
        key_all,
        value_all,
    )

    hops = REDUCE_CUTS * sum(hops for _, _, hops in reduce_plan(zs))
    cut = 4 * tokens // REDUCE_CUTS
    ranks = rank // 2
    lanes = shard + 128
    chunk = (ranks + ranks // min(zs, 4), shard // zs)
    copies = hops + 9 + 1 + 6 + 3 + 2 * (zs - 1) + 1
    query_grad, value_grad, input_gradient, down_share, up_share = pl.pallas_call(
        functools.partial(finish_kernel, zs),
        out_shape=(
            shape((tokens, QUERY_HEADS * HEAD_SIZE), bf16),
            shape((tokens, kv_width), bf16),
            shape((tokens, model), bf16),
            shape((rank, shard), f32),
            shape((rank, adapter_up.shape[1]), f32),
        ),
        in_specs=[VMEM, ANY, VMEM, VMEM, HBM, HBM],
        out_specs=(ANY, ANY, VMEM, VMEM, VMEM),
        scratch_shapes=[
            pltpu.VMEM((2, zs) + chunk, f32),
            pltpu.VMEM((hops, cut, HEAD_SIZE), bf16),
            pltpu.VMEM((hops, cut, HEAD_SIZE), bf16),
            pltpu.VMEM((2, 4 * tokens, HEAD_SIZE), bf16),
            pltpu.VMEM((tokens, kv_width), bf16),
            pltpu.VMEM((tokens, model), bf16),
            pltpu.VMEM((model, packed_width), bf16),
            pltpu.VMEM((tokens, packed_width), bf16),
            pltpu.VMEM((8, 2, ranks, lanes), bf16),
            pltpu.VMEM((8, ranks, lanes), bf16),
            pltpu.VMEM((8, ranks, lanes), bf16),
            pltpu.VMEM((2, ranks, lanes), bf16),
            pltpu.VMEM((2, ranks, lanes), bf16),
            pltpu.VMEM((2, 2, ranks, lanes), bf16),
            pltpu.VMEM((2, ranks, lanes), bf16),
            pltpu.VMEM((3, ranks, lanes), bf16),
            pltpu.VMEM((zs,) + chunk, f32),
            pltpu.VMEM((zs - 1,) + chunk, f32),
            dma(copies),
            dma(copies),
            dma(5),
        ],
        compiler_params=params(44, 1),
        name="sum_gradients",
    )(partial_sums, query_grad_group, low_rank, complete_up, rows_in, full)

    return (query_grad[None], value_grad[None], input_gradient[None], down_share.T, up_share)


def solution(mesh):
    spread, rows = P("fsdp", "context", None), P("fsdp", None)
    placed = (spread, spread, spread, spread, rows, rows, P(None, "fsdp"), rows, rows)
    return jax.shard_map(
        functools.partial(body, mesh.shape["context"] // 4),
        mesh=mesh,
        in_specs=placed,
        out_specs=(spread, spread, spread, rows, P(None, "fsdp")),
        check_vma=False,
    )
```

```python
import functools
import math

import jax
import jax.numpy as jnp
from jax import lax
from jax.experimental import pallas as pl
from jax.experimental.pallas import tpu as pltpu
from jax.sharding import PartitionSpec as P

QUERY_HEADS = 32
KEY_VALUE_HEADS = 4
HEAD_SIZE = 128
GROUPS = QUERY_HEADS // KEY_VALUE_HEADS
SPAN = 64
ADAPTER_SCALE = 0.5
NEGATIVE_FILL = -1e30
KEY_TILE = 256
MESH = pl.DeviceIdType.MESH
ANY = pl.BlockSpec(memory_space=pl.ANY)
VMEM = pl.BlockSpec(memory_space=pltpu.VMEM)
HBM = pl.BlockSpec(memory_space=pltpu.HBM)
SMEM = pl.BlockSpec(memory_space=pltpu.SMEM)


def at(start, size):
    return pl.ds(pl.multiple_of(start, size), size)


class Place:
    def __init__(self, zs):
        self.zs = zs
        self.fsdp = lax.axis_index("fsdp")
        self.context = lax.axis_index("context")
        self.y_hi, self.x = lax.div(self.fsdp, 4), lax.rem(self.fsdp, 4)
        self.z, self.member = lax.div(self.context, 4), lax.rem(self.context, 4)
        self.y_lo, self.core = lax.div(self.member, 2), lax.rem(self.member, 2)

    def row(self, y_hi, x):
        return y_hi * 4 + lax.rem(x, 4)

    def at_x(self, step):
        return {"fsdp": self.row(self.y_hi, self.x + step), "context": self.context}

    def across_y(self):
        return {
            "fsdp": self.row(1 - self.y_hi, self.x),
            "context": self.z * 4 + (1 - self.y_lo) * 2 + self.core,
        }

    def other_y_lo(self):
        return self.of_context(self.z * 4 + (1 - self.y_lo) * 2 + self.core)

    def sibling(self):
        return self.of_context(self.z * 4 + self.y_lo * 2 + 1 - self.core)

    def of_context(self, context):
        return {"fsdp": self.fsdp, "context": context}

    def fellow(self, k):
        return lax.rem(self.member + k, 4)

    def at_fellow(self, k):
        return self.of_context(self.z * 4 + self.fellow(k))

    def z_at(self, step):
        return lax.rem(self.z + step + self.zs, self.zs)

    def at_z(self, step):
        return self.of_context(self.z_at(step) * 4 + self.member)


def greet(partners):
    barrier = pltpu.get_barrier_semaphore()
    for partner in partners:
        pl.semaphore_signal(barrier, inc=1, device_id=partner, device_id_type=MESH)
    pl.semaphore_wait(barrier, len(partners))


class Sender:
    def __init__(self, send_sems, recv_sems):
        self.send_sems, self.recv_sems, self.copies = send_sems, recv_sems, []

    def send(self, src, dst, device):
        k = len(self.copies)
        assert k < self.send_sems.shape[0]
        copy = pltpu.make_async_remote_copy(
            src_ref=src,
            dst_ref=dst,
            send_sem=self.send_sems.at[k],
            recv_sem=self.recv_sems.at[k],
            device_id=device,
            device_id_type=MESH,
        )
        copy.start()
        self.copies.append(copy)
        return copy

    def finish(self):
        for copy in self.copies:
            copy.wait_send()


class Ring:
    def __init__(self, place, sender, buffer, block, rows):
        self.place, self.sender, self.buffer = place, sender, buffer
        self.block, self.rows, self.stage, self.flying = block, rows, 0, ()
        self.stages = place.zs // 2

    def step(self):
        for copy in self.flying:
            copy.wait_recv()
        self.flying = ()
        if self.stage == self.stages:
            return
        right_at, left_at = self.block(self.place.z_at(-self.stage)), self.block(self.place.z_at(self.stage))
        if self.stage < self.stages - 1:
            right_rows, left_rows = at(right_at, self.rows), at(left_at, self.rows)
        else:
            cut = self.rows // 2
            right_rows, left_rows = at(right_at, cut), at(left_at + cut, cut)
        buffer, send = self.buffer, self.sender.send
        self.flying = (
            send(buffer.at[right_rows], buffer.at[right_rows], self.place.at_z(1)),
            send(buffer.at[left_rows], buffer.at[left_rows], self.place.at_z(-1)),
        )
        self.stage += 1

    def run(self):
        while self.stage < self.stages or self.flying:
            self.step()


def keys_kernel(
    zs,
    w_hbm,
    d_ref,
    u_ref,
    x_hbm,
    q_ref,
    g_ref,
    v_ref,
    full_ref,
    qg_ref,
    gg_ref,
    vg_ref,
    kg_ref,
    low_ref,
    up_ref,
    full,
    inputs,
    projected,
    pair_in,
    keys,
    send_sems,
    recv_sems,
    own_sems,
):
    place = Place(zs)
    tokens = q_ref.shape[0]
    shard, kv_width = w_hbm.shape
    rank = d_ref.shape[0]
    unit = shard // 8
    width = GROUPS * HEAD_SIZE
    member = place.member
    mine = at((place.z * 4 + member) * tokens, tokens)
    columns = at(member * HEAD_SIZE, HEAD_SIZE)
    piece = shard // 2

    def columns_of(f, core):
        return at(f * shard + core * piece, piece)

    def own_inputs(f):
        return pltpu.make_async_copy(
            x_hbm.at[:, columns_of(f, place.core)],
            inputs.at[:tokens, f * piece : (f + 1) * piece],
            own_sems.at[0],
        )

    for f in range(8):
        own_inputs(f).start()
    owns = [
        pltpu.make_async_copy(
            q_ref.at[:, at(member * width, width)], qg_ref.at[at(member * tokens, tokens)], own_sems.at[1]
        ),
        pltpu.make_async_copy(
            g_ref.at[:, at(member * width, width)], gg_ref.at[at(member * tokens, tokens)], own_sems.at[2]
        ),
        pltpu.make_async_copy(v_ref.at[:, columns], vg_ref.at[mine], own_sems.at[3]),
    ]
    for own in owns:
        own.start()
    own_rows = at(place.fsdp * shard, shard)
    weights = pltpu.make_async_copy(w_hbm, full.at[own_rows, :kv_width], own_sems.at[5])
    weights.start()
    filler = jnp.zeros((shard // 2 - rank, u_ref.shape[1]), jnp.bfloat16)
    up_rows = jnp.concatenate([u_ref[...], filler] * 2, axis=0)
    full[own_rows, kv_width:] = jnp.concatenate([d_ref[...].T, up_rows], axis=1)
    projected[...] = jnp.zeros_like(projected)
    weights.wait()

    right, left, across, sibling = place.at_x(1), place.at_x(3), place.across_y(), place.sibling()
    z_up, z_down = place.at_z(1), place.at_z(-1)
    greet([right, left, across] + [place.at_fellow(k) for k in (1, 2, 3)] + [z_up, z_down])
    sender = Sender(send_sems, recv_sems)
    send = sender.send

    parity = lax.rem(place.z, 2)

    def rows_of(f, offset, size):
        begin = f * shard + place.core * 4 * unit + offset
        return full.at[pl.ds(pl.multiple_of(begin, unit // 2), size)]

    def bridge(f):
        return rows_of(f, parity * 3 * unit, unit)

    def body(f):
        return rows_of(f, unit, 2 * unit)

    def low_body(f):
        return rows_of(f, unit, unit // 2)

    def high_body(f):
        return rows_of(f, unit + unit // 2, 3 * unit // 2)

    def pass_on(block, *devices):
        return [send(block, block, device) for device in devices]

    y_hi, x = place.y_hi, place.x
    row = lambda y, step: place.row(y, x + step)
    own, near_left, near_right, far = (row(y_hi, k) for k in (0, 3, 1, 2))
    over, over_left, over_right, over_far = (row(1 - y_hi, k) for k in (0, 3, 1, 2))

    sibling_inputs = [
        send(
            x_hbm.at[:, columns_of(f, 1 - place.core)],
            inputs.at[tokens:, f * piece : (f + 1) * piece],
            sibling,
        )
        for f in range(8)
    ]
    value_copies = [
        send(
            v_ref.at[:, at(place.fellow(k) * HEAD_SIZE, HEAD_SIZE)], vg_ref.at[mine], place.at_fellow(k)
        )
        for k in (1, 2, 3)
    ]
    near_left_bridge, near_right_bridge, over_bridge = pass_on(bridge(own), right, left, across)
    near_left_body, near_right_body, over_body = pass_on(body(own), right, left, across)
    shares = {}
    crossing = {}

    def share(name, f):
        shares[name] = pass_on(rows_of(f, parity * unit, 3 * unit), sibling)[0]

    def cross(name, f):
        begin = parity * 3 * unit
        crossing[name] = (
            pass_on(rows_of(f, begin, unit // 2), z_up)
            + pass_on(rows_of(f, begin + unit // 2, unit // 2), z_down)
        )

    def land(name, f):
        for copy in crossing[name]:
            copy.wait_recv()
        shares[name, "rest"] = pass_on(rows_of(f, (1 - parity) * 3 * unit, unit), sibling)[0]

    def multiply(f, offset, size):
        columns = pl.ds(pl.multiple_of(f * piece + offset, unit), size)
        projected[...] += jnp.dot(
            inputs[:, columns], rows_of(f, offset, size)[...], preferred_element_type=jnp.float32
        )

    def project(f):
        multiply(f, parity * unit, 3 * unit)

    def project_rest(f):
        multiply(f, (1 - parity) * 3 * unit, unit)

    pltpu.make_async_copy(x_hbm.at[:, : 8 * piece], inputs.at[:tokens], own_sems.at[0]).wait()
    for copy in sibling_inputs:
        copy.wait_recv()
    multiply(own, 0, 4 * unit)

    near_left_bridge.wait_recv()
    far_bridge = pass_on(bridge(near_left), right)[0]
    cross("near_left", near_left)
    near_right_bridge.wait_recv()
    cross("near_right", near_right)
    over_bridge.wait_recv()
    over_left_bridge, over_right_bridge = pass_on(bridge(over), right, left)
    cross("over", over)
    head_copies = []
    for k in (2, 3, 1):
        for src, dst in ((q_ref, qg_ref), (g_ref, gg_ref)):
            head_copies.append(
                send(
                    src.at[:, at(place.fellow(k) * width, width)],
                    dst.at[at(member * tokens, tokens)],
                    place.at_fellow(k),
                )
            )

    near_left_body.wait_recv()
    far_low = pass_on(low_body(near_left), right)[0]
    near_right_body.wait_recv()
    far_high = pass_on(high_body(near_right), left)[0]
    over_body.wait_recv()
    over_left_body, over_right_body = pass_on(body(over), right, left)
    share("near_left", near_left)
    share("near_right", near_right)
    share("over", over)
    far_bridge.wait_recv()
    over_far_bridge = pass_on(bridge(far), across)[0]
    cross("far", far)
    far_low.wait_recv()
    over_far_low = pass_on(low_body(far), across)[0]
    for name, f in (("near_left", near_left), ("near_right", near_right), ("over", over)):
        land(name, f)
    far_high.wait_recv()
    over_far_high = pass_on(high_body(far), across)[0]
    share("far", far)
    for copy in value_copies:
        copy.wait_recv()
    owns[2].wait()
    ring = Ring(place, sender, vg_ref, lambda z: z * 4 * tokens, 4 * tokens)
    ring.step()
    over_left_bridge.wait_recv()
    cross("over_left", over_left)
    over_right_bridge.wait_recv()
    cross("over_right", over_right)
    over_far_bridge.wait_recv()
    cross("over_far", over_far)
    land("far", far)
    for f in (near_left, near_right, over, far):
        project(f)
        project_rest(f)
    over_left_body.wait_recv()
    project(over_left)
    share("over_left", over_left)
    over_right_body.wait_recv()
    project(over_right)
    share("over_right", over_right)
    ring.step()
    for name, f in (("over_left", over_left), ("over_right", over_right), ("over_far", over_far)):
        land(name, f)
        project_rest(f)
    over_far_low.wait_recv()
    over_far_high.wait_recv()
    project(over_far)
    pair_copy = send(projected.at[tokens:], pair_in, sibling)
    share("over_far", over_far)

    def stores(core):
        for f in range(8):
            rows = columns_of(f, core)
            pltpu.make_async_copy(full.at[rows], full_ref.at[rows], own_sems.at[0]).start()

    stores(place.core)
    ring.step()
    pair_copy.wait_recv()
    projection = projected[:tokens] + pair_in[...]

    low_rank = projection[:, kv_width : kv_width + rank].astype(jnp.bfloat16)
    low_ref[...] = low_rank
    for f in range(8):
        up_ref[:, f * (kv_width // 8) : (f + 1) * (kv_width // 8)] = full[
            at(f * shard + place.core * piece, rank), kv_width + rank :
        ]
    keys[...] = (
        projection[:, :kv_width]
        + ADAPTER_SCALE * jnp.dot(low_rank, up_ref[...], preferred_element_type=jnp.float32)
    ).astype(jnp.bfloat16)
    own_keys = pltpu.make_async_copy(keys.at[:, columns], kg_ref.at[mine], own_sems.at[4])
    own_keys.start()

    def exchange(device, fellow):
        return send(keys.at[:, at(fellow * HEAD_SIZE, HEAD_SIZE)], kg_ref.at[mine], device)

    to_sibling = exchange(sibling, member + 1 - 2 * place.core)
    other = [
        exchange(place.at_fellow(k), place.fellow(k)) for k in (2,)
    ]
    third = lax.rem(member + 3 - 2 * place.core, 4)
    other.append(exchange(place.of_context(place.z * 4 + third), third))
    rings = [
        Ring(place, sender, kg_ref, lambda z: (z * 4 + place.y_lo * 2) * tokens, 2 * tokens),
        Ring(place, sender, kg_ref, lambda z: (z * 4 + (1 - place.y_lo) * 2) * tokens, 2 * tokens),
    ]
    to_sibling.wait_recv()
    own_keys.wait()
    rings[0].step()
    for copy in other:
        copy.wait_recv()
    rings[1].step()
    rings.append(ring)
    ring.step()
    for some in rings:
        some.step()
    for copy in shares.values():
        copy.wait_recv()
    stores(1 - place.core)
    while any(some.flying for some in rings):
        for some in rings:
            some.step()
    for copy in head_copies:
        copy.wait_recv()
    sender.finish()
    owns[0].wait()
    owns[1].wait()
    pltpu.make_async_copy(full, full_ref, own_sems.at[0]).wait()


def attention_kernel(
    zs,
    list_ref,
    doc_smem,
    doc_ref,
    queries,
    gradients,
    k_ref,
    v_ref,
    dq_hbm,
    dkv_ref,
    keys,
    values,
    totals,
    scores,
    grads,
    dq_rows,
    q_columns,
    g_columns,
    firsts,
    starts,
    store_sem,
):
    to_exponent = math.log2(math.e) / math.sqrt(HEAD_SIZE)
    inv_root = 1.0 / math.sqrt(HEAD_SIZE)
    lanes = GROUPS * SPAN
    spans = list_ref.shape[0]
    own_spans = queries.shape[0] // SPAN
    z = lax.div(lax.axis_index("context"), 4)
    length = spans * SPAN

    keys[length:, :] = jnp.zeros((KEY_TILE, HEAD_SIZE), jnp.bfloat16)
    values[length:, :] = jnp.zeros((KEY_TILE, HEAD_SIZE), jnp.bfloat16)

    @pl.loop(0, spans + KEY_TILE // SPAN)
    def _(n):
        totals[at(n * SPAN, SPAN), :] = jnp.zeros((SPAN, 2 * HEAD_SIZE), jnp.float32)

    def document_start(position):
        document = doc_smem[0, position]

        def narrow(_, carry):
            low, high = carry
            middle = lax.shift_right_logical(low + high, 1)
            earlier = doc_smem[0, middle] < document
            return jnp.where(earlier, middle + 1, low), jnp.where(earlier, high, middle)

        return lax.fori_loop(0, 12, narrow, (jnp.maximum(position - 1024, 0), position))[0]

    shape = (own_spans, 2 * SPAN)
    row = lax.broadcasted_iota(jnp.int32, shape, 0)
    lane = lax.broadcasted_iota(jnp.int32, shape, 1)
    row_begin, row_first = jnp.zeros(shape, jnp.int32), jnp.zeros(shape, jnp.int32)
    for i in range(own_spans):
        slot = list_ref[z * own_spans + i]
        begin = lax.shift_right_logical(slot, 1) * 2 * SPAN
        starts[i : i + 1, :] = doc_ref[0:1, pl.ds(pl.multiple_of(begin, 2 * SPAN), 2 * SPAN)]
        row_begin = jnp.where(row == i, begin, row_begin)
        row_first = jnp.where(row == i, document_start(begin), row_first)
        firsts[i] = lax.shift_right_logical(document_start(slot * SPAN), 6)
    documents = starts[...]
    changes = jnp.where((lane > 0) & (documents != pltpu.roll(documents, 1, 1)), lane, 0)
    for step in (1, 2, 4, 8, 16, 32, 64):
        changes = jnp.maximum(changes, jnp.where(lane >= step, pltpu.roll(changes, step, 1), 0))
    starts[...] = jnp.where(changes == 0, row_first, row_begin + changes)

    @pl.loop(0, spans)
    def _(s):
        src, dst = at(s * SPAN, SPAN), at(list_ref[s] * SPAN, SPAN)
        keys[dst, :] = k_ref[src, :]
        values[dst, :] = v_ref[src, :]

    @pl.loop(0, own_spans)
    def _(i):
        slot, first = list_ref[z * own_spans + i], firsts[i]
        own = at(i * SPAN, SPAN)
        q_rows = jnp.concatenate(
            [queries[own, g * HEAD_SIZE : (g + 1) * HEAD_SIZE] for g in range(GROUPS)], axis=0
        )
        g_rows = jnp.concatenate(
            [gradients[own, g * HEAD_SIZE : (g + 1) * HEAD_SIZE] for g in range(GROUPS)], axis=0
        )
        pair = starts[pl.ds(i, 1), :]
        own_start = jnp.where(lax.rem(slot, 2) == 1, pair[:, SPAN:], pair[:, :SPAN])
        q_columns[...] = q_rows.T
        g_columns[...] = g_rows.T
        q_start = jnp.concatenate([own_start] * GROUPS, axis=1) - first * SPAN
        lane = lax.broadcasted_iota(jnp.int32, (1, lanes), 1)
        q_pos = (slot - first) * SPAN + lax.rem(lane, SPAN)
        tiles = lax.div(slot - first + KEY_TILE // SPAN, KEY_TILE // SPAN)

        def rows_at(t, first=first):
            return pl.ds(pl.multiple_of(first * SPAN + t * KEY_TILE, SPAN), KEY_TILE)

        def peak_step(t, peak, q_rows=q_rows, q_start=q_start, q_pos=q_pos, rows_at=rows_at):
            raw = jnp.dot(keys[rows_at(t), :], q_columns[...], preferred_element_type=jnp.float32)
            key_pos = lax.broadcasted_iota(jnp.int32, (KEY_TILE, lanes), 0)
            raw = jnp.where(
                (key_pos >= q_start - t * KEY_TILE) & (key_pos <= q_pos - t * KEY_TILE), raw, NEGATIVE_FILL
            )
            scores[t] = raw
            grads[t] = jnp.dot(values[rows_at(t), :], g_columns[...], preferred_element_type=jnp.float32)
            return jnp.maximum(peak, jnp.max(raw, axis=0, keepdims=True))

        peak = lax.fori_loop(0, tiles, peak_step, jnp.full((1, lanes), NEGATIVE_FILL, jnp.float32))

        def sum_step(t, carry, peak=peak):
            normalizer, weighted = carry
            weights = jnp.exp2((scores[t] - peak) * to_exponent)
            scores[t] = weights
            return (
                normalizer + jnp.sum(weights, axis=0, keepdims=True),
                weighted + jnp.sum(weights * grads[t], axis=0, keepdims=True),
            )

        zero = jnp.zeros((1, lanes), jnp.float32)
        normalizer, weighted = lax.fori_loop(0, tiles, sum_step, (zero, zero))
        inverse = 1.0 / normalizer
        row_terms = weighted * inverse

        def grad_step(t, dq, q_rows=q_rows, g_rows=g_rows, inverse=inverse, row_terms=row_terms, rows_at=rows_at):
            rows = rows_at(t)
            probability = scores[t] * inverse
            dscore = (probability * (grads[t] - row_terms) * inv_root).astype(jnp.bfloat16)
            prob_low = probability.astype(jnp.bfloat16)
            totals[rows, :HEAD_SIZE] += jnp.dot(dscore, q_rows, preferred_element_type=jnp.float32)
            totals[rows, HEAD_SIZE:] += jnp.dot(prob_low, g_rows, preferred_element_type=jnp.float32)
            return dq + lax.dot_general(
                keys[rows, :], dscore, (((0,), (0,)), ((), ())), preferred_element_type=jnp.float32
            )

        dq = lax.fori_loop(0, tiles, grad_step, jnp.zeros((HEAD_SIZE, lanes), jnp.float32))
        dq = dq.T.astype(jnp.bfloat16)
        for g in range(GROUPS):
            dq_rows[own, g * HEAD_SIZE : (g + 1) * HEAD_SIZE] = dq[g * SPAN : (g + 1) * SPAN]
        pltpu.make_async_copy(dq_rows.at[own], dq_hbm.at[own], store_sem).start()

    @pl.loop(0, spans)
    def _(s):
        dkv_ref[at(s * SPAN, SPAN), :] = totals[at(list_ref[s] * SPAN, SPAN), :].astype(jnp.bfloat16)

    pltpu.make_async_copy(dq_rows, dq_hbm, store_sem).wait()


REDUCE_CUTS = 2


def reduce_plan(zs):
    half = zs // 2
    return [(1, 0, half), (-1, 1, half), (-1, 0, half - 1), (1, 1, half - 1)]


def finish_kernel(
    zs,
    dkv_ref,
    dqg_ref,
    low_ref,
    up_ref,
    x_hbm,
    full_hbm,
    dq_ref,
    vg_ref,
    grad_ref,
    down_ref,
    up_out,
    total_ref,
    out,
    held,
    done,
    key_grad,
    inputs,
    full,
    stacked,
    parts,
    pair_in,
    row,
    far_in,
    near_out,
    near_in,
    y_out,
    y_in,
    z_out,
    z_in,
    send_sems,
    recv_sems,
    own_sems,
):
    place = Place(zs)
    tokens = dq_ref.shape[0]
    width = GROUPS * HEAD_SIZE
    member = place.member
    rows = 4 * tokens
    cut = rows // REDUCE_CUTS
    loads = [
        pltpu.make_async_copy(x_hbm, inputs, own_sems.at[0]),
        pltpu.make_async_copy(full_hbm, full, own_sems.at[1]),
    ]
    for load in loads:
        load.start()
    own_query = pltpu.make_async_copy(
        dqg_ref.at[at(member * tokens, tokens)], dq_ref.at[:, at(member * width, width)], own_sems.at[2]
    )
    own_query.start()
    right, left, across = place.at_x(1), place.at_x(3), place.across_y()
    sibling, other_lo = place.sibling(), place.other_y_lo()
    beyond = {"fsdp": place.row(1 - place.y_hi, place.x), "context": place.context}
    greet(
        [place.at_fellow(k) for k in (1, 2, 3)]
        + [place.at_z(k) for k in range(1, zs)]
        + [right, left, across, beyond]
    )
    sender = Sender(send_sems, recv_sems)
    send = sender.send

    plan = reduce_plan(zs)
    last = {}
    slot = 0
    query_copies = []
    for step in range(zs // 2):
        for piece in range(REDUCE_CUTS):
            for chain, (direction, column, hops) in enumerate(plan):
                if step >= hops:
                    continue
                columns = slice(column * HEAD_SIZE, (column + 1) * HEAD_SIZE)
                destination = place.z_at(direction * (hops - step))
                mine = dkv_ref[at(destination * rows + piece * cut, cut), columns]
                if step > 0:
                    copy, before = last[chain, piece]
                    copy.wait_recv()
                    mine = (mine.astype(jnp.float32) + held[before].astype(jnp.float32)).astype(jnp.bfloat16)
                out[slot] = mine
                last[chain, piece] = (send(out.at[slot], held.at[slot], place.at_z(direction)), slot)
                slot += 1
        if step == 0:
            for k in (2, 3, 1):
                query_copies.append(
                    send(
                        dqg_ref.at[at(place.fellow(k) * tokens, tokens)],
                        dq_ref.at[:, at(member * width, width)],
                        place.at_fellow(k),
                    )
                )
    owns, key_copies, value_copies = [], [], []
    for column, target, copies in ((0, key_grad, key_copies), (1, vg_ref, value_copies)):
        columns = slice(column * HEAD_SIZE, (column + 1) * HEAD_SIZE)
        for piece in range(REDUCE_CUTS):
            total = dkv_ref[at(place.z * rows + piece * cut, cut), columns].astype(jnp.float32)
            for chain, (direction, its_column, hops) in enumerate(plan):
                if its_column == column and hops:
                    copy, before = last[chain, piece]
                    copy.wait_recv()
                    total = total + held[before].astype(jnp.float32)
            done[column, piece * cut : (piece + 1) * cut, :] = total.astype(jnp.bfloat16)
        landing = target.at[:, at(member * HEAD_SIZE, HEAD_SIZE)]
        own = pltpu.make_async_copy(
            done.at[column, at(member * tokens, tokens)], landing, own_sems.at[3 + column]
        )
        own.start()
        owns.append(own)
        for k in (2, 3, 1):
            copies.append(
                send(done.at[column, at(place.fellow(k) * tokens, tokens)], landing, place.at_fellow(k))
            )
    loads[0].wait()
    owns[0].wait()
    for copy in key_copies:
        copy.wait_recv()

    kg = key_grad[...]
    lifted = lax.dot_general(
        kg, up_ref[...], (((1,), (1,)), ((), ())), preferred_element_type=jnp.float32
    ).astype(jnp.bfloat16)
    scaled = (lifted.astype(jnp.float32) * ADAPTER_SCALE).astype(jnp.bfloat16)
    rank = lifted.shape[1]
    ranks = rank // 2
    kv_width = kg.shape[1]
    stacked[:, :kv_width] = kg
    stacked[:, kv_width:] = jnp.concatenate([scaled, jnp.zeros_like(scaled)], axis=1)
    up_part = (
        ADAPTER_SCALE
        * lax.dot_general(low_ref[...], kg, (((0,), (0,)), ((), ())), preferred_element_type=jnp.float32)
    ).astype(jnp.bfloat16)
    lanes = parts.shape[3] - 128
    share = kv_width // 8
    padding = jnp.zeros((rank, 128 - share), jnp.bfloat16)
    for f in range(8):
        block = jnp.concatenate([up_part[:, f * share : (f + 1) * share], padding], axis=1)
        parts[f, 0, :, lanes:] = block[:ranks]
        parts[f, 1, :, lanes:] = block[ranks:]

    @pl.loop(0, 8)
    def _(f):
        block = lax.dot_general(
            scaled, inputs[:, at(f * lanes, lanes)], (((0,), (0,)), ((), ())), preferred_element_type=jnp.float32
        ).astype(jnp.bfloat16)
        parts[f, 0, :, :lanes] = block[:ranks]
        parts[f, 1, :, :lanes] = block[ranks:]

    pair_copy = send(parts.at[:, 1 - place.core], pair_in, sibling)
    loads[1].wait()

    def input_gradient(begin, end):
        @pl.loop(begin, end)
        def _(j):
            some = at(j * lanes, lanes)
            grad_ref[:, some] = lax.dot_general(
                stacked[...], full[some, :], (((1,), (1,)), ((), ())), preferred_element_type=jnp.float32
            ).astype(jnp.bfloat16)

    input_gradient(0, 2)
    pair_copy.wait_recv()

    def add(*terms):
        total = terms[0].astype(jnp.float32)
        for term in terms[1:]:
            total = total + term.astype(jnp.float32)
        return total

    @pl.loop(0, 8)
    def _(f):
        row[f] = add(parts[f, pl.ds(place.core, 1)][0], pair_in[f]).astype(jnp.bfloat16)

    here = lambda y_hi, step: place.row(y_hi, place.x + step)
    far_copies = [
        send(row.at[here(0, 2)], far_in.at[0], right),
        send(row.at[here(1, 2)], far_in.at[1], left),
    ]
    near_copies = [
        send(row.at[here(1, 1)], near_in.at[0, 1], right),
        send(row.at[here(0, 3)], near_in.at[1, 0], left),
    ]
    input_gradient(2, 3)
    for way, (y_hi, step, device) in enumerate(((0, 1, right), (1, 3, left))):
        far_copies[way].wait_recv()
        near_out[way] = add(row[here(y_hi, step)], far_in[way]).astype(jnp.bfloat16)
        near_copies.append(send(near_out.at[way], near_in.at[way, y_hi], device))
    input_gradient(3, 5)
    for copy in near_copies:
        copy.wait_recv()

    def over_x(y_hi):
        return add(row[here(y_hi, 0)], near_in[0, y_hi], near_in[1, y_hi])

    y_out[0] = over_x(1 - place.y_hi).astype(jnp.bfloat16)
    y_copies = [send(y_out.at[0], y_in.at[0], beyond), send(y_out.at[0], y_in.at[1], across)]
    mine = over_x(place.y_hi)
    y_out[1] = mine.astype(jnp.bfloat16)
    y_copies.append(send(y_out.at[1], y_in.at[2], other_lo))
    input_gradient(5, 6)
    for copy in y_copies:
        copy.wait_recv()
    mine = add(mine, y_in[0], y_in[1], y_in[2])
    chunk_lanes = lanes // zs
    cuts = min(zs, 4)
    small = ranks // cuts
    for j in range(zs):
        z_out[j, :ranks] = mine[:, j * chunk_lanes : (j + 1) * chunk_lanes]
        z_out[j, ranks:] = mine[(j % cuts) * small : (j % cuts + 1) * small, lanes:]
    z_copies = []
    for k in sorted(range(1, zs), key=lambda k: -min(k, zs - k)):
        z_copies.append(send(z_out.at[place.z_at(k)], z_in.at[k - 1], place.at_z(k)))
    input_gradient(6, 7)
    for copy in z_copies:
        copy.wait_recv()
    chunk = z_out[place.z]
    for k in range(zs - 1):
        chunk = chunk + z_in[k]
    total_ref[pl.ds(place.core, 1), pl.ds(place.z, 1)] = chunk[None, None]
    block = total_ref.at[place.core, place.z]
    z_copies = []
    for k in sorted(range(1, zs), key=lambda k: -min(k, zs - k)):
        z_copies.append(send(block, block, place.at_z(k)))
    input_gradient(7, 8)
    for copy in z_copies:
        copy.wait_recv()
    block = total_ref.at[place.core]
    send(block, block, sibling).wait_recv()
    for core in range(2):
        for j in range(zs):
            down_ref[core * ranks : (core + 1) * ranks, j * chunk_lanes : (j + 1) * chunk_lanes] = total_ref[
                core, j, :ranks
            ]
        for j in range(cuts):
            begin = core * ranks + j * small
            up_out[begin : begin + small, :] = total_ref[core, j, ranks:, :share]
    for copy in value_copies + query_copies:
        copy.wait_recv()
    sender.finish()
    owns[1].wait()
    own_query.wait()


def dma(count):
    return pltpu.SemaphoreType.DMA((count,))


def params(mebibytes, collective_id=None):
    if collective_id is None:
        return pltpu.CompilerParams(vmem_limit_bytes=mebibytes << 20)
    return pltpu.CompilerParams(
        vmem_limit_bytes=mebibytes << 20, collective_id=collective_id, has_side_effects=True
    )


def body(
    zs,
    inputs,
    queries,
    values,
    output_gradient,
    key_base_weight,
    adapter_down,
    adapter_up,
    span_slot_index,
    segment_document,
):
    bf16, f32, i32 = jnp.bfloat16, jnp.float32, jnp.int32
    rows_in = inputs[0]
    tokens, model = rows_in.shape
    shard, kv_width = key_base_weight.shape
    rank = adapter_down.shape[1]
    length = segment_document.shape[1]
    width = GROUPS * HEAD_SIZE
    half = zs // 2
    shape = jax.ShapeDtypeStruct
    packed_width = kv_width + rank + adapter_up.shape[1]

    copies = 9 + 3 + 6 + 6 + 3 + 4 + 3 + 7 * 4 + 3 + 3 * 2 * half
    full, query_group, gradient_group, value_all, key_all, low_rank, complete_up = pl.pallas_call(
        functools.partial(keys_kernel, zs),
        out_shape=(
            shape((model, packed_width), bf16),
            shape((4 * tokens, width), bf16),
            shape((4 * tokens, width), bf16),
            shape((length, HEAD_SIZE), bf16),
            shape((length, HEAD_SIZE), bf16),
            shape((tokens, rank), bf16),
            shape((rank, kv_width), bf16),
        ),
        in_specs=[ANY, VMEM, VMEM, ANY, ANY, ANY, ANY],
        out_specs=(ANY,) + (VMEM,) * 6,
        scratch_shapes=[
            pltpu.VMEM((model, packed_width), bf16),
            pltpu.VMEM((2 * tokens, model // 2), bf16),
            pltpu.VMEM((2 * tokens, packed_width), f32),
            pltpu.VMEM((tokens, packed_width), f32),
            pltpu.VMEM((tokens, kv_width), bf16),
            dma(copies),
            dma(copies),
            dma(6),
        ],
        compiler_params=params(48, 0),
        name="gather_weights_and_keys",
    )(
        key_base_weight,
        adapter_down.T,
        adapter_up,
        rows_in,
        queries[0],
        output_gradient[0],
        values[0],
    )

    span_rows = 4 * tokens
    tile_rows = (1024 // KEY_TILE + 1, KEY_TILE, GROUPS * SPAN)
    query_grad_group, partial_sums = pl.pallas_call(
        functools.partial(attention_kernel, zs),
        out_shape=(
            jax.ShapeDtypeStruct((span_rows, width), bf16),
            jax.ShapeDtypeStruct((length, 2 * HEAD_SIZE), bf16),
        ),
        in_specs=[SMEM, SMEM] + [VMEM] * 5,
        out_specs=(ANY, VMEM),
        scratch_shapes=[
            pltpu.VMEM((length + KEY_TILE, HEAD_SIZE), bf16),
            pltpu.VMEM((length + KEY_TILE, HEAD_SIZE), bf16),
            pltpu.VMEM((length + KEY_TILE, 2 * HEAD_SIZE), f32),
            pltpu.VMEM(tile_rows, f32),
            pltpu.VMEM(tile_rows, f32),
            pltpu.VMEM((span_rows, width), bf16),
            pltpu.VMEM((HEAD_SIZE, GROUPS * SPAN), bf16),
            pltpu.VMEM((HEAD_SIZE, GROUPS * SPAN), bf16),
            pltpu.SMEM((span_rows // SPAN,), i32),
            pltpu.VMEM((span_rows // SPAN, 2 * SPAN), i32),
            pltpu.SemaphoreType.DMA,
        ],
        compiler_params=params(24),
        name="attention_gradients",
    )(
        span_slot_index[0],
        segment_document,
        segment_document,
        query_group,
        gradient_group,
        key_all,
        value_all,
    )

    hops = REDUCE_CUTS * sum(hops for _, _, hops in reduce_plan(zs))
    cut = 4 * tokens // REDUCE_CUTS
    ranks = rank // 2
    lanes = shard + 128
    chunk = (ranks + ranks // min(zs, 4), shard // zs)
    copies = hops + 9 + 1 + 6 + 3 + 2 * (zs - 1) + 1
    query_grad, value_grad, input_gradient, down_share, up_share = pl.pallas_call(
        functools.partial(finish_kernel, zs),
        out_shape=(
            shape((tokens, QUERY_HEADS * HEAD_SIZE), bf16),
            shape((tokens, kv_width), bf16),
            shape((tokens, model), bf16),
            shape((rank, shard), f32),
            shape((rank, adapter_up.shape[1]), f32),
        ),
        in_specs=[VMEM, ANY, VMEM, VMEM, HBM, HBM],
        out_specs=(ANY, ANY, VMEM, VMEM, VMEM),
        scratch_shapes=[
            pltpu.VMEM((2, zs) + chunk, f32),
            pltpu.VMEM((hops, cut, HEAD_SIZE), bf16),
            pltpu.VMEM((hops, cut, HEAD_SIZE), bf16),
            pltpu.VMEM((2, 4 * tokens, HEAD_SIZE), bf16),
            pltpu.VMEM((tokens, kv_width), bf16),
            pltpu.VMEM((tokens, model), bf16),
            pltpu.VMEM((model, packed_width), bf16),
            pltpu.VMEM((tokens, packed_width), bf16),
            pltpu.VMEM((8, 2, ranks, lanes), bf16),
            pltpu.VMEM((8, ranks, lanes), bf16),
            pltpu.VMEM((8, ranks, lanes), bf16),
            pltpu.VMEM((2, ranks, lanes), bf16),
            pltpu.VMEM((2, ranks, lanes), bf16),
            pltpu.VMEM((2, 2, ranks, lanes), bf16),
            pltpu.VMEM((2, ranks, lanes), bf16),
            pltpu.VMEM((3, ranks, lanes), bf16),
            pltpu.VMEM((zs,) + chunk, f32),
            pltpu.VMEM((zs - 1,) + chunk, f32),
            dma(copies),
            dma(copies),
            dma(5),
        ],
        compiler_params=params(44, 1),
        name="sum_gradients",
    )(partial_sums, query_grad_group, low_rank, complete_up, rows_in, full)

    return (query_grad[None], value_grad[None], input_gradient[None], down_share.T, up_share)


def solution(mesh):
    spread, rows = P("fsdp", "context", None), P("fsdp", None)
    placed = (spread, spread, spread, spread, rows, rows, P(None, "fsdp"), rows, rows)
    return jax.shard_map(
        functools.partial(body, mesh.shape["context"] // 4),
        mesh=mesh,
        in_specs=placed,
        out_specs=(spread, spread, spread, rows, P(None, "fsdp")),
        check_vma=False,
    )
```
